512 devices in a mesh: chan: 16 (over x_lo, y), tm: 32 (over z, x_hi, core).
Axes of the slice: x: 4 (x_hi: 2, x_lo: 2; x = x_hi * 2 + x_lo), y: 8, z: 8, core: 2. Of those that a mesh axis runs over, the one named last changes fastest.
Arguments:
- samples: bfloat16 [1024, 262144], P('chan', 'tm'), may hold values from -6 to 6
- cell_of_feed: int32 [1024], replicated, may hold values from 0 to 1023, each once
Outputs:
- beam_power: float32 [32, 1024, 1024], P('tm', 'chan')
The draws below stay inside these ranges and needn't reach their ends.
Inputs may be any that keep to these rules, and one draw needn't show every extreme that they name: `cell_of_feed`: each grid cell is named by exactly one feed.
All inputs are finite; a program needn't handle non-finite values.
Results may differ from the reference program's by a relative error of at most 0.0019.
Values may be sent and summed in bfloat16 or wider, within the bound.
A program may use at most 64 MiB of HBM per device.

```python
import math
import jax
import jax.numpy as jnp
from jax import lax

POSN = 256
CYL = 4
NFFT = 2048
TAPS = 4
TSUM = 4
INPUTS = 1024
BEAMS = 1024
CHANS = 1024
SAMPLES = 262144
TOUT = 32


def block_levels(rng, shape, pieces, least, largest):
    gain, own = 1.0, jax.random.fold_in(rng, 6)
    for position, shards_of in pieces:
        heights = jnp.exp(jax.random.uniform(jax.random.fold_in(own, position), (shards_of,), jnp.float32, least / len(pieces), largest / len(pieces)))
        gain = gain * jnp.repeat(heights, shape[position] // shards_of).reshape([-1 if axis == position else 1 for axis in range(len(shape))])
    return gain


def bell_draw(own_key, shape, spread, limit, split=(), kind=jnp.bfloat16):
    gain = block_levels(own_key, shape, split, -0.22, 0.18) if split else 1.0
    values = jax.random.normal(own_key, shape, jnp.float32) * spread * gain
    return jnp.minimum(jnp.maximum(values, -limit), limit).astype(kind)


def setup_inputs(seed: int = 0) -> dict:
    key_list = jax.random.split(jax.random.key(seed), 3)
    return {
        "samples": bell_draw(key_list[0], (INPUTS, SAMPLES), 1.0, 6.0, ((0, 16), (1, 32))),
        "cell_of_feed": jax.random.permutation(key_list[1], INPUTS).astype(jnp.int32),
    }


def pfb_window():
    offsets = jnp.arange(TAPS * NFFT, dtype=jnp.float32) + 0.5
    shaped = jnp.sinc(offsets / NFFT - TAPS / 2.0)
    tapered = 0.5 - 0.5 * jnp.cos(offsets * (2.0 * math.pi / (TAPS * NFFT)))
    return (shaped * tapered).reshape(TAPS, NFFT)

def reference(samples, cell_of_feed):
    history = TAPS - 1
    window = pfb_window()

    def one_block(block_index):
        first_sample = (block_index * (TSUM * NFFT)).astype(jnp.int32)
        current = lax.dynamic_slice_in_dim(samples, first_sample, TSUM * NFFT, 1).astype(jnp.float32)
        earlier_start = jnp.maximum(first_sample - history * NFFT, 0).astype(jnp.int32)
        earlier = lax.dynamic_slice_in_dim(samples, earlier_start, history * NFFT, 1).astype(jnp.float32)
        earlier = earlier * (block_index > 0).astype(jnp.float32)
        extended = jnp.concatenate([earlier, current], axis=1).reshape(INPUTS, TSUM + history, NFFT)
        summed = window[0] * extended[:, 0:TSUM]
        for tap_index in range(1, TAPS):
            summed = summed + window[tap_index] * extended[:, tap_index:tap_index + TSUM]
        spectrum = jnp.fft.rfft(summed, axis=-1)[..., :CHANS] / math.sqrt(NFFT)
        real_part = spectrum.real.astype(jnp.bfloat16)
        imag_part = spectrum.imag.astype(jnp.bfloat16)
        grid_real = jnp.zeros_like(real_part).at[cell_of_feed].set(real_part)
        grid_imag = jnp.zeros_like(imag_part).at[cell_of_feed].set(imag_part)
        grid_real, grid_imag = lax.optimization_barrier((grid_real, grid_imag))
        voltage = grid_real.astype(jnp.float32) + 1j * grid_imag.astype(jnp.float32)
        voltage = voltage.reshape(CYL, POSN, TSUM, CHANS)
        beam_field = jnp.fft.fft2(voltage, axes=(0, 1))
        energy = lax.optimization_barrier(jnp.sum(beam_field.real ** 2 + beam_field.imag ** 2, axis=2)) / (TSUM * INPUTS)
        return energy.reshape(BEAMS, CHANS)
    return lax.map(one_block, jnp.arange(TOUT, dtype=jnp.int32))
```

```python
import functools
import math

import jax
import jax.numpy as jnp
import ml_dtypes
import numpy as np
from jax import lax
from jax.experimental import pallas as pl
from jax.experimental.pallas import tpu as pltpu
from jax.sharding import PartitionSpec as P

POSN = 256
CYL = 4
NFFT = 2048
TAPS = 4
TSUM = 4
INPUTS = 1024

STEP = 16
FINE = NFFT // STEP
HALF = FINE // 2
HISTORY = TAPS - 1

BF16 = jnp.bfloat16
F32 = jnp.float32
MESH = pl.DeviceIdType.MESH


def two_parts(table):
    high = table.astype(ml_dtypes.bfloat16)
    low = (table - high.astype(np.float64)).astype(ml_dtypes.bfloat16)
    return np.stack([high, low])


def window_table():
    offsets = np.arange(TAPS * NFFT) + 0.5
    shaped = np.sinc(offsets / NFFT - TAPS / 2.0)
    tapered = 0.5 - 0.5 * np.cos(offsets * (2.0 * math.pi / (TAPS * NFFT)))
    return (shaped * tapered).reshape(TAPS, NFFT).astype(np.float32)


def channel_tables():
    b = np.arange(FINE)[:, None]
    j = np.arange(HALF)[None, :]

    def waves(s):
        angle = 2.0 * math.pi * ((b * (STEP * j + s)) % NFFT) / NFFT
        return np.cos(angle), np.sin(angle)

    out = np.zeros((STEP // 2, 2 * FINE, 2 * FINE))
    for half, s in enumerate((0, STEP // 2)):
        cos, sin = waves(s)
        out[0, half * FINE : (half + 1) * FINE, half * FINE : (half + 1) * FINE] = np.concatenate([cos, -sin], 1)
    for p in range(1, STEP // 2):
        cos, sin = waves(p)
        out[p, :FINE, :FINE] = np.concatenate([cos, -sin], 1)
        out[p, FINE:, :FINE] = np.concatenate([sin, cos], 1)
        cos, sin = waves(STEP - p)
        out[p, :FINE, FINE:] = np.concatenate([cos, -sin], 1)
        out[p, FINE:, FINE:] = np.concatenate([-sin, -cos], 1)
    return two_parts(out / math.sqrt(NFFT))


def position_tables():
    v = np.arange(POSN)
    angle = 2.0 * math.pi * ((v[:, None] * v[None, :]) % POSN) / POSN
    return two_parts(np.concatenate([np.cos(angle), np.sin(angle)], 1))


def short_dft(x):
    c1, c2, c3 = (math.cos(math.pi * n / 8) for n in (1, 2, 3))
    s = [x[a] + x[a + 8] for a in range(8)]
    d = [x[a] - x[a + 8] for a in range(8)]
    ss = [s[a] + s[a + 4] for a in range(4)]
    sd = [s[a] - s[a + 4] for a in range(4)]
    p0, p1 = ss[0] + ss[2], ss[1] + ss[3]
    t1, t2 = c2 * (sd[1] - sd[3]), c2 * (sd[1] + sd[3])
    f = [None] + [d[a] - d[8 - a] for a in (1, 2, 3)]
    g = [None] + [d[a] + d[8 - a] for a in (1, 2, 3)]
    cf, cg = c2 * f[2], c2 * g[2]
    even, odd = d[0] + cf, d[0] - cf
    pp, qq = c1 * f[1] + c3 * f[3], c3 * f[1] - c1 * f[3]
    vv, ww = c3 * g[1] + c1 * g[3], c1 * g[1] - c3 * g[3]
    ee, ff = cg + d[4], cg - d[4]
    return [
        (p0 + p1, p0 - p1),
        (even + pp, -(vv + ee)),
        (sd[0] + t1, -(sd[2] + t2)),
        (odd + qq, -(ww + ff)),
        (ss[0] - ss[2], ss[3] - ss[1]),
        (odd - qq, ff - ww),
        (sd[0] - t1, sd[2] - t2),
        (even - pp, ee - vv),
    ]


def dot(left, right):
    return jnp.dot(left, right, preferred_element_type=F32)


def kernel(
    peers,
    blocks,
    samples,
    cell,
    window_in,
    channel_in,
    position_in,
    out,
    frames,
    window,
    channel,
    position,
    terms,
    outgoing,
    spectra,
    choose,
    along,
    energy,
    packed,
    arrived,
    ordered,
    load_sem,
    halo_send,
    halo_recv,
    spectra_send,
    spectra_recv,
    power_send,
    power_recv,
):
    me = lax.axis_index("chan")
    block = lax.axis_index("tm")
    after = lax.rem(block + 1, blocks)
    before = lax.rem(block + blocks - 1, blocks)

    def peer(k):
        return lax.rem(me + k, peers)

    barrier = pltpu.get_barrier_semaphore()
    pl.semaphore_signal(barrier, inc=1, device_id={"tm": before}, device_id_type=MESH)

    def greet(k, carry):
        pl.semaphore_signal(barrier, inc=1, device_id={"chan": peer(k)}, device_id_type=MESH)
        return carry

    lax.fori_loop(1, peers, greet, 0)

    loads = [
        pltpu.make_async_copy(samples.at[:, pl.ds(q * NFFT, NFFT)], frames.at[HISTORY + q], load_sem.at[q])
        for q in range(TSUM)
    ]
    loads.append(pltpu.make_async_copy(window_in, window, load_sem.at[4]))
    loads.append(pltpu.make_async_copy(channel_in, channel, load_sem.at[5]))
    loads.append(pltpu.make_async_copy(position_in, position, load_sem.at[6]))
    for load in loads:
        load.start()

    def halo(f):
        return pltpu.make_async_remote_copy(
            src_ref=samples.at[:, pl.ds((f + 1) * NFFT, NFFT)],
            dst_ref=frames.at[f],
            send_sem=halo_send.at[f],
            recv_sem=halo_recv.at[f],
            device_id={"tm": after},
            device_id_type=MESH,
        )

    def spectra_copy(t, source, target, k, slot):
        return pltpu.make_async_remote_copy(
            src_ref=outgoing.at[t, source],
            dst_ref=spectra.at[t, slot],
            send_sem=spectra_send.at[t, k],
            recv_sem=spectra_recv.at[t, slot],
            device_id={"chan": target},
            device_id_type=MESH,
        )

    def power_copy(source, target, k, slot):
        return pltpu.make_async_remote_copy(
            src_ref=packed.at[source],
            dst_ref=arrived.at[slot],
            send_sem=power_send.at[k],
            recv_sem=power_recv.at[slot],
            device_id={"chan": target},
            device_id_type=MESH,
        )

    def filter_frame(t):
        def rows_of(r, carry):
            rows = pl.ds(pl.multiple_of(r * 16, 16), 16)
            x = []
            for a in range(STEP):
                lanes = pl.ds(a * FINE, FINE)
                total = None
                for k in range(TAPS):
                    term = window[pl.ds(k, 1), lanes] * frames[t + k, rows, lanes].astype(F32)
                    total = term if total is None else total + term
                x.append(total)
            for p, pair in enumerate(short_dft(x)):
                for part, value in enumerate(pair):
                    lanes = pl.ds(part * FINE, FINE)
                    high = value.astype(BF16)
                    terms[p, rows, lanes] = high
                    terms[p, pl.ds(pl.multiple_of(64 + r * 16, 16), 16), lanes] = (value - high.astype(F32)).astype(BF16)
            return carry

        lax.fori_loop(0, 4, rows_of, 0)

    def channelize(t):
        for p in range(STEP // 2):
            first = dot(terms[p], channel[0, p])
            second = dot(terms[p, pl.ds(0, 64), :], channel[1, p])
            result = (first[:64] + first[64:] + second).astype(BF16)
            outgoing[t, p] = result[:, :FINE]
            outgoing[t, 8 if p == 0 else STEP - p] = result[:, FINE:]

    def send_spectra(t):
        def one(k, carry):
            spectra_copy(t, peer(k), peer(k), k, me).start()
            return carry

        lax.fori_loop(1, peers, one, 0)
        spectra[t, me] = outgoing[t, me]

    for load in loads[:6]:
        load.wait()
    filter_frame(TSUM - 1)
    channelize(TSUM - 1)
    pl.semaphore_wait(barrier, peers)
    for f in (2, 1, 0):
        halo(f).start()
    send_spectra(TSUM - 1)

    def choose_rows(r, carry):
        first = pl.multiple_of(r * 32, 32)
        number = lax.broadcasted_iota(jnp.int32, (32, INPUTS), 0) + first
        choose[pl.ds(first, 32), :] = jnp.where(number == cell[...], 1.0, 0.0).astype(BF16)
        return carry

    lax.fori_loop(0, INPUTS // 32, choose_rows, 0)

    def later_frame(step, carry):
        t = TSUM - 1 - step
        halo(t).wait_recv()

        @pl.when(block == 0)
        def _():
            frames[t] = jnp.zeros((64, NFFT), BF16)

        filter_frame(t)
        channelize(t)
        send_spectra(t)
        return carry

    lax.fori_loop(1, TSUM, later_frame, 0)

    loads[6].wait()
    lane = lax.broadcasted_iota(jnp.int32, (1, FINE), 1)
    left = lane < HALF
    sign = jnp.where(left, 1.0, -1.0)

    def turned(value):
        return pltpu.roll(value, HALF, 1) * sign

    def beams_of(pair, carry):
        for t in (2 * pair, 2 * pair + 1):

            def landed(k, inner, t=t):
                spectra_copy(t, me, me, k, peer(k)).wait_recv()
                return inner

            lax.fori_loop(1, peers, landed, 0)
        received = jnp.concatenate(
            [spectra[2 * pair + n].reshape(INPUTS, FINE) for n in range(2)], axis=1
        )
        for g in range(CYL):
            placed = dot(choose[pl.ds(g * POSN, POSN), :], received)
            swapped = jnp.concatenate([turned(placed[:, :FINE]), turned(placed[:, FINE:])], axis=1)
            both = jnp.concatenate([placed, swapped], axis=0).astype(BF16)
            along[g] = dot(position[0], both) + dot(position[1], both)

        def power_rows(r, inner):
            rows = pl.ds(pl.multiple_of(r * 16, 16), 16)
            squares = [None] * CYL
            for n in range(2):
                a = [along[g, rows, pl.ds(n * FINE, FINE)] for g in range(CYL)]
                even, odd = a[0] + a[2], a[1] + a[3]
                across, quarter = a[0] - a[2], turned(a[1] - a[3])
                for u, beam in enumerate((even + odd, across + quarter, even - odd, across - quarter)):
                    squares[u] = beam * beam if n == 0 else squares[u] + beam * beam
            for u in range(CYL):
                energy[u, rows, :] += squares[u]
            return inner

        lax.fori_loop(0, POSN // 16, power_rows, 0)
        return carry

    energy[...] = jnp.zeros_like(energy)
    beams_of(1, 0)
    beams_of(0, 0)

    for duo in range(2):
        for side in range(2):
            rows = pl.ds(side * 128, 128)
            one, two = energy[2 * duo, rows, :], energy[2 * duo + 1, rows, :]
            both = jnp.where(left, one, two) + pltpu.roll(jnp.where(left, two, one), HALF, 1)
            upright = (both * (1.0 / (TSUM * INPUTS))).T
            for u in range(2):
                low = upright[u * HALF : u * HALF + 32]
                high = upright[u * HALF + 32 : u * HALF + 64]
                target = (2 * duo + u) * 4 + 2 * side
                packed[target] = jnp.where(left, low, pltpu.roll(high, HALF, 1))
                packed[target + 1] = jnp.where(left, pltpu.roll(low, HALF, 1), high)

    def send_power(k, carry):
        power_copy(peer(k), peer(k), k, me).start()
        return carry

    lax.fori_loop(1, peers, send_power, 0)
    arrived[me] = packed[me]

    def settle(k, carry):
        for t in range(TSUM):
            spectra_copy(t, peer(k), peer(k), k, me).wait_send()
        power_copy(peer(k), peer(k), k, me).wait_send()
        return carry

    for f in range(HISTORY):
        halo(f).wait_send()
    lax.fori_loop(1, peers, settle, 0)

    def power_landed(k, carry):
        power_copy(me, me, k, peer(k)).wait_recv()
        return carry

    lax.fori_loop(1, peers, power_landed, 0)
    for s in range(STEP):
        ordered[pl.ds(s, 32, stride=STEP), :] = arrived[s]
    for q in range(4):
        upright = ordered[pl.ds(q * 128, 128), :].T
        out[:, pl.ds(q * 128, 128)] = upright[:HALF]
        out[:, pl.ds(512 + q * 128, 128)] = upright[HALF:]


def local(peers, blocks, samples, cell_of_feed):
    vmem = pl.BlockSpec(memory_space=pltpu.VMEM)
    anywhere = pl.BlockSpec(memory_space=pl.ANY)
    dma = pltpu.SemaphoreType.DMA
    power = pl.pallas_call(
        functools.partial(kernel, peers, blocks),
        out_shape=jax.ShapeDtypeStruct((64, 1024), F32),
        in_specs=[anywhere, vmem, anywhere, anywhere, anywhere],
        out_specs=vmem,
        scratch_shapes=[
            pltpu.VMEM((HISTORY + TSUM, 64, NFFT), BF16),
            pltpu.VMEM((TAPS, NFFT), F32),
            pltpu.VMEM((2, STEP // 2, 2 * FINE, 2 * FINE), BF16),
            pltpu.VMEM((2, POSN, 2 * POSN), BF16),
            pltpu.VMEM((STEP // 2, 128, 2 * FINE), BF16),
            pltpu.VMEM((TSUM, peers, 64, FINE), BF16),
            pltpu.VMEM((TSUM, peers, 64, FINE), BF16),
            pltpu.VMEM((INPUTS, INPUTS), BF16),
            pltpu.VMEM((CYL, POSN, 2 * FINE), F32),
            pltpu.VMEM((CYL, POSN, FINE), F32),
            pltpu.VMEM((peers, 32, 128), F32),
            pltpu.VMEM((peers, 32, 128), F32),
            pltpu.VMEM((512, 128), F32),
            dma((7,)),
            dma((HISTORY,)),
            dma((HISTORY,)),
            dma((TSUM, peers)),
            dma((TSUM, peers)),
            dma((peers,)),
            dma((peers,)),
        ],
        compiler_params=pltpu.CompilerParams(
            collective_id=0, has_side_effects=True, vmem_limit_bytes=60 * 1024 * 1024
        ),
    )(
        samples,
        cell_of_feed.reshape(1, INPUTS),
        jnp.asarray(window_table()),
        jnp.asarray(channel_tables()),
        jnp.asarray(position_tables()),
    )
    return power.reshape(1, 64, 1024)


def solution(mesh):
    return jax.shard_map(
        functools.partial(local, mesh.shape["chan"], mesh.shape["tm"]),
        mesh=mesh,
        in_specs=(P("chan", "tm"), P()),
        out_specs=P("tm", "chan", None),
        check_vma=False,
    )
```

```python
import functools
import math

import jax
import jax.numpy as jnp
import ml_dtypes
import numpy as np
from jax import lax
from jax.experimental import pallas as pl
from jax.experimental.pallas import tpu as pltpu
from jax.sharding import PartitionSpec as P

POSN = 256
CYL = 4
NFFT = 2048
TAPS = 4
TSUM = 4
INPUTS = 1024

STEP = 16
FINE = NFFT // STEP
HALF = FINE // 2
HISTORY = TAPS - 1

BF16 = jnp.bfloat16
F32 = jnp.float32
MESH = pl.DeviceIdType.MESH


def two_parts(table):
    high = table.astype(ml_dtypes.bfloat16)
    low = (table - high.astype(np.float64)).astype(ml_dtypes.bfloat16)
    return np.stack([high, low])


def window_table():
    offsets = np.arange(TAPS * NFFT) + 0.5
    shaped = np.sinc(offsets / NFFT - TAPS / 2.0)
    tapered = 0.5 - 0.5 * np.cos(offsets * (2.0 * math.pi / (TAPS * NFFT)))
    return (shaped * tapered).reshape(TAPS, NFFT).astype(np.float32)


def channel_tables():
    b = np.arange(FINE)[:, None]
    j = np.arange(HALF)[None, :]

    def waves(s):
        angle = 2.0 * math.pi * ((b * (STEP * j + s)) % NFFT) / NFFT
        return np.cos(angle), np.sin(angle)

    out = np.zeros((STEP // 2, 2 * FINE, 2 * FINE))
    for half, s in enumerate((0, STEP // 2)):
        cos, sin = waves(s)
        out[0, half * FINE : (half + 1) * FINE, half * FINE : (half + 1) * FINE] = np.concatenate([cos, -sin], 1)
    for p in range(1, STEP // 2):
        cos, sin = waves(p)
        out[p, :FINE, :FINE] = np.concatenate([cos, -sin], 1)
        out[p, FINE:, :FINE] = np.concatenate([sin, cos], 1)
        cos, sin = waves(STEP - p)
        out[p, :FINE, FINE:] = np.concatenate([cos, -sin], 1)
        out[p, FINE:, FINE:] = np.concatenate([-sin, -cos], 1)
    return two_parts(out / math.sqrt(NFFT))


def position_tables():
    v = np.arange(POSN)
    angle = 2.0 * math.pi * ((v[:, None] * v[None, :]) % POSN) / POSN
    return two_parts(np.concatenate([np.cos(angle), np.sin(angle)], 1))


def short_dft(x):
    c1, c2, c3 = (math.cos(math.pi * n / 8) for n in (1, 2, 3))
    s = [x[a] + x[a + 8] for a in range(8)]
    d = [x[a] - x[a + 8] for a in range(8)]
    ss = [s[a] + s[a + 4] for a in range(4)]
    sd = [s[a] - s[a + 4] for a in range(4)]
    p0, p1 = ss[0] + ss[2], ss[1] + ss[3]
    t1, t2 = c2 * (sd[1] - sd[3]), c2 * (sd[1] + sd[3])
    f = [None] + [d[a] - d[8 - a] for a in (1, 2, 3)]
    g = [None] + [d[a] + d[8 - a] for a in (1, 2, 3)]
    cf, cg = c2 * f[2], c2 * g[2]
    even, odd = d[0] + cf, d[0] - cf
    pp, qq = c1 * f[1] + c3 * f[3], c3 * f[1] - c1 * f[3]
    vv, ww = c3 * g[1] + c1 * g[3], c1 * g[1] - c3 * g[3]
    ee, ff = cg + d[4], cg - d[4]
    return [
        (p0 + p1, p0 - p1),
        (even + pp, -(vv + ee)),
        (sd[0] + t1, -(sd[2] + t2)),
        (odd + qq, -(ww + ff)),
        (ss[0] - ss[2], ss[3] - ss[1]),
        (odd - qq, ff - ww),
        (sd[0] - t1, sd[2] - t2),
        (even - pp, ee - vv),
    ]


def dot(left, right):
    return jnp.dot(left, right, preferred_element_type=F32)


def kernel(
    peers,
    blocks,
    samples,
    cell_in,
    window_in,
    channel_in,
    position_in,
    arrived,
    scale_in,
    frames,
    cell,
    window,
    channel,
    position,
    terms,
    outgoing,
    spectra,
    choose,
    along,
    energy,
    packed,
    scale_out,
    load_sem,
    halo_send,
    halo_recv,
    spectra_send,
    spectra_recv,
    power_send,
    power_recv,
    scale_send,
    scale_recv,
):
    me = lax.axis_index("chan")
    block = lax.axis_index("tm")
    is_first, is_last = block == 0, block == blocks - 1

    def peer(k):
        return lax.rem(me + k, peers)

    def drained(ref, sem):
        pltpu.make_async_copy(ref, ref, sem).wait()

    barrier = pltpu.get_barrier_semaphore()

    @pl.when(jnp.logical_not(is_first))
    def _():
        pl.semaphore_signal(barrier, inc=1, device_id={"tm": block - 1}, device_id_type=MESH)

    def greet(k, carry):
        pl.semaphore_signal(barrier, inc=1, device_id={"chan": peer(k)}, device_id_type=MESH)
        return carry

    lax.fori_loop(1, peers, greet, 0)

    for q in range(TSUM):
        pltpu.make_async_copy(
            samples.at[:, pl.ds(q * NFFT, NFFT)], frames.at[HISTORY + q], load_sem.at[0]
        ).start()
    loads = [
        pltpu.make_async_copy(source, target, load_sem.at[n + 1])
        for n, (source, target) in enumerate(
            ((window_in, window), (channel_in, channel), (position_in, position), (cell_in, cell))
        )
    ]
    for load in loads:
        load.start()

    def halo(f):
        return pltpu.make_async_remote_copy(
            src_ref=samples.at[:, pl.ds((f + 1) * NFFT, NFFT)],
            dst_ref=frames.at[f],
            send_sem=halo_send,
            recv_sem=halo_recv.at[f],
            device_id={"tm": block + 1},
            device_id_type=MESH,
        )

    def spectra_copy(t, target):
        return pltpu.make_async_remote_copy(
            src_ref=outgoing.at[t, target],
            dst_ref=spectra.at[t, me],
            send_sem=spectra_send,
            recv_sem=spectra_recv.at[t],
            device_id={"chan": target},
            device_id_type=MESH,
        )

    def power_copy(target):
        return pltpu.make_async_remote_copy(
            src_ref=packed.at[target],
            dst_ref=arrived.at[me],
            send_sem=power_send,
            recv_sem=power_recv,
            device_id={"chan": target},
            device_id_type=MESH,
        )

    def scale_copy(target):
        return pltpu.make_async_remote_copy(
            src_ref=scale_out.at[target],
            dst_ref=scale_in.at[me],
            send_sem=scale_send,
            recv_sem=scale_recv,
            device_id={"chan": target},
            device_id_type=MESH,
        )

    def filter_frame(t):
        def rows_of(r, carry):
            rows = pl.ds(pl.multiple_of(r * 16, 16), 16)
            x = []
            for a in range(STEP):
                lanes = pl.ds(a * FINE, FINE)
                total = None
                for k in range(TAPS):
                    term = window[pl.ds(k, 1), lanes] * frames[t + k, rows, lanes].astype(F32)
                    total = term if total is None else total + term
                x.append(total)
            for p, pair in enumerate(short_dft(x)):
                for part, value in enumerate(pair):
                    lanes = pl.ds(part * FINE, FINE)
                    high = value.astype(BF16)
                    terms[p, rows, lanes] = high
                    terms[p, pl.ds(pl.multiple_of(64 + r * 16, 16), 16), lanes] = (value - high.astype(F32)).astype(BF16)
            return carry

        lax.fori_loop(0, 4, rows_of, 0)

    def channelize(t):
        for p in range(STEP // 2):
            first = dot(terms[p], channel[0, p])
            second = dot(terms[p, pl.ds(0, 64), :], channel[1, p])
            result = (first[:64] + first[64:] + second).astype(BF16)
            outgoing[t, p] = result[:, :FINE]
            outgoing[t, 8 if p == 0 else STEP - p] = result[:, FINE:]

    def send_spectra(t):
        def one(k, carry):
            spectra_copy(t, peer(k)).start()
            return carry

        lax.fori_loop(1, peers, one, 0)
        spectra[t, me] = outgoing[t, me]

    drained(frames.at[pl.ds(HISTORY, TSUM)], load_sem.at[0])
    loads[0].wait()
    filter_frame(TSUM - 1)
    loads[1].wait()
    channelize(TSUM - 1)
    pl.semaphore_wait(barrier, jnp.where(is_last, peers - 1, peers))

    @pl.when(jnp.logical_not(is_last))
    def _():
        for f in (2, 1, 0):
            halo(f).start()

    send_spectra(TSUM - 1)

    loads[3].wait()

    def choose_rows(r, carry):
        first = pl.multiple_of(r * 32, 32)
        number = lax.broadcasted_iota(jnp.int32, (32, INPUTS), 0) + first
        choose[pl.ds(first, 32), :] = jnp.where(number == cell[...], 1.0, 0.0).astype(BF16)
        return carry

    lax.fori_loop(0, INPUTS // 32, choose_rows, 0)

    def later_frame(step, carry):
        t = TSUM - 1 - step

        @pl.when(jnp.logical_not(is_first))
        def _():
            halo(t).wait_recv()

        @pl.when(is_first)
        def _():
            frames[t] = jnp.zeros((64, NFFT), BF16)

        filter_frame(t)
        channelize(t)
        send_spectra(t)
        return carry

    lax.fori_loop(1, TSUM, later_frame, 0)

    loads[2].wait()
    lane = lax.broadcasted_iota(jnp.int32, (1, FINE), 1)
    left = lane < HALF
    sign = jnp.where(left, 1.0, -1.0)

    def turned(value):
        return pltpu.roll(value, HALF, 1) * sign

    def beams_of(t):
        drained(spectra.at[t, pl.ds(0, peers - 1)], spectra_recv.at[t])
        received = spectra[t].reshape(INPUTS, FINE)
        for g in range(CYL):
            placed = dot(choose[pl.ds(g * POSN, POSN), :], received)
            both = jnp.concatenate([placed, turned(placed)], axis=0).astype(BF16)
            along[g] = dot(position[0], both) + dot(position[1], both)

    def power_of(first):
        def power_rows(r, carry):
            rows = pl.ds(pl.multiple_of(r * 32, 32), 32)
            a = [along[g, rows, :] for g in range(CYL)]
            even, odd = a[0] + a[2], a[1] + a[3]
            across, quarter = a[0] - a[2], turned(a[1] - a[3])
            squares = [beam * beam for beam in (even + odd, across + quarter, even - odd, across - quarter)]
            for duo in range(2):
                one, two = squares[2 * duo], squares[2 * duo + 1]
                folded = jnp.where(left, one, two) + pltpu.roll(jnp.where(left, two, one), HALF, 1)
                energy[duo, rows, :] = folded if first else energy[duo, rows, :] + folded
            return carry

        lax.fori_loop(0, POSN // 32, power_rows, 0, unroll=2)

    beams_of(TSUM - 1)
    power_of(True)

    def more_beams(step, carry):
        beams_of(TSUM - 1 - step)
        power_of(False)
        return carry

    lax.fori_loop(1, TSUM, more_beams, 0)

    largest = jnp.max(jnp.max(jnp.maximum(energy[0], energy[1]), axis=0, keepdims=True), axis=1, keepdims=True)
    largest = jnp.maximum(largest, 1e-36)
    scale_out[...] = jnp.broadcast_to((largest * (1.0 / (TSUM * INPUTS))).reshape(1, 1, 1), (peers, 1, 128))
    inverse = 1.0 / largest

    for duo in range(2):
        for side in range(2):
            share = energy[duo, pl.ds(side * 128, 128), :] * inverse
            share = share * share
            upright = (share * share).T
            for u in range(2):
                low = upright[u * HALF : u * HALF + 32]
                high = upright[u * HALF + 32 : u * HALF + 64]
                target = (2 * duo + u) * 4 + 2 * side
                packed[target] = jnp.where(left, low, pltpu.roll(high, HALF, 1)).astype(BF16)
                packed[target + 1] = jnp.where(left, pltpu.roll(low, HALF, 1), high).astype(BF16)

    def send_power(k, carry):
        scale_copy(peer(k)).start()
        power_copy(peer(k)).start()
        return carry

    lax.fori_loop(1, peers, send_power, 0)
    arrived[me] = packed[me]
    scale_in[me] = scale_out[me]

    @pl.when(jnp.logical_not(is_last))
    def _():
        drained(frames.at[pl.ds(0, HISTORY)], halo_send)

    others = pl.ds(0, peers - 1)
    drained(outgoing.at[:, others], spectra_send)
    drained(packed.at[others], power_send)
    drained(scale_out.at[others], scale_send)
    drained(arrived.at[others], power_recv)
    drained(scale_in.at[others], scale_recv)


def interleave(arrived, scale, out, ordered):
    for s in range(STEP):
        ordered[pl.ds(s, 32, stride=STEP), :] = lax.rsqrt(lax.rsqrt(arrived[s].astype(F32))) * scale[s]
    for q in range(4):
        upright = ordered[pl.ds(q * 128, 128), :].T
        out[:, pl.ds(q * 128, 128)] = upright[:HALF]
        out[:, pl.ds(512 + q * 128, 128)] = upright[HALF:]


def local(peers, blocks, samples, cell_of_feed):
    vmem = pl.BlockSpec(memory_space=pltpu.VMEM)
    anywhere = pl.BlockSpec(memory_space=pl.ANY)
    dma = pltpu.SemaphoreType.DMA
    arrived, scale = pl.pallas_call(
        functools.partial(kernel, peers, blocks),
        out_shape=(
            pltpu.VMEM((peers, 32, 128), BF16),
            pltpu.VMEM((peers, 1, 128), F32),
        ),
        in_specs=[anywhere] * 5,
        out_specs=(vmem, vmem),
        scratch_shapes=[
            pltpu.VMEM((HISTORY + TSUM, 64, NFFT), BF16),
            pltpu.VMEM((1, INPUTS), jnp.int32),
            pltpu.VMEM((TAPS, NFFT), F32),
            pltpu.VMEM((2, STEP // 2, 2 * FINE, 2 * FINE), BF16),
            pltpu.VMEM((2, POSN, 2 * POSN), BF16),
            pltpu.VMEM((STEP // 2, 128, 2 * FINE), BF16),
            pltpu.VMEM((TSUM, peers, 64, FINE), BF16),
            pltpu.VMEM((TSUM, peers, 64, FINE), BF16),
            pltpu.VMEM((INPUTS, INPUTS), BF16),
            pltpu.VMEM((CYL, POSN, FINE), F32),
            pltpu.VMEM((2, POSN, FINE), F32),
            pltpu.VMEM((peers, 32, 128), BF16),
            pltpu.VMEM((peers, 1, 128), F32),
            dma((5,)),
            dma(()),
            dma((HISTORY,)),
            dma(()),
            dma((TSUM,)),
            dma(()),
            dma(()),
            dma(()),
            dma(()),
        ],
        compiler_params=pltpu.CompilerParams(
            collective_id=0, has_side_effects=True, vmem_limit_bytes=60 * 1024 * 1024
        ),
    )(
        samples,
        cell_of_feed.reshape(1, INPUTS),
        jnp.asarray(window_table()),
        jnp.asarray(channel_tables()),
        jnp.asarray(position_tables()),
    )
    power = pl.pallas_call(
        interleave,
        out_shape=jax.ShapeDtypeStruct((64, 1024), F32),
        in_specs=[vmem, vmem],
        out_specs=vmem,
        scratch_shapes=[pltpu.VMEM((512, 128), F32)],
    )(arrived, scale)
    return power.reshape(1, 64, 1024)


def solution(mesh):
    return jax.shard_map(
        functools.partial(local, mesh.shape["chan"], mesh.shape["tm"]),
        mesh=mesh,
        in_specs=(P("chan", "tm"), P()),
        out_specs=P("tm", "chan", None),
        check_vma=False,
    )
```

```python
import functools
import math

import jax
import jax.numpy as jnp
import ml_dtypes
import numpy as np
from jax import lax
from jax.experimental import pallas as pl
from jax.experimental.pallas import tpu as pltpu
from jax.sharding import PartitionSpec as P

POSN = 256
CYL = 4
NFFT = 2048
TAPS = 4
TSUM = 4
INPUTS = 1024

STEP = 16
FINE = NFFT // STEP
HALF = FINE // 2
HISTORY = TAPS - 1

BF16 = jnp.bfloat16
F32 = jnp.float32
MESH = pl.DeviceIdType.MESH


def two_parts(table):
    high = table.astype(ml_dtypes.bfloat16)
    low = (table - high.astype(np.float64)).astype(ml_dtypes.bfloat16)
    return np.stack([high, low])


def window_table():
    offsets = np.arange(TAPS * NFFT) + 0.5
    shaped = np.sinc(offsets / NFFT - TAPS / 2.0)
    tapered = 0.5 - 0.5 * np.cos(offsets * (2.0 * math.pi / (TAPS * NFFT)))
    return (shaped * tapered).reshape(TAPS, NFFT).astype(np.float32)


def channel_tables():
    b = np.arange(FINE)[:, None]
    j = np.arange(HALF)[None, :]

    def waves(s):
        angle = 2.0 * math.pi * ((b * (STEP * j + s)) % NFFT) / NFFT
        return np.cos(angle), np.sin(angle)

    out = np.zeros((STEP // 2, 2 * FINE, 2 * FINE))
    for half, s in enumerate((0, STEP // 2)):
        cos, sin = waves(s)
        out[0, half * FINE : (half + 1) * FINE, half * FINE : (half + 1) * FINE] = np.concatenate([cos, -sin], 1)
    for p in range(1, STEP // 2):
        cos, sin = waves(p)
        out[p, :FINE, :FINE] = np.concatenate([cos, -sin], 1)
        out[p, FINE:, :FINE] = np.concatenate([sin, cos], 1)
        cos, sin = waves(STEP - p)
        out[p, :FINE, FINE:] = np.concatenate([cos, -sin], 1)
        out[p, FINE:, FINE:] = np.concatenate([-sin, -cos], 1)
    return two_parts(out / math.sqrt(NFFT))


def position_tables():
    v, r = np.arange(POSN // 2)[:, None], np.arange(POSN // 2)[None, :]
    out = []
    for odd in range(2):
        angle = 2.0 * math.pi * ((v * (2 * r + odd)) % POSN) / POSN
        out.append(np.concatenate(two_parts(np.concatenate([np.cos(angle), np.sin(angle)], 1))))
    return np.stack(out)


def short_dft(x):
    c1, c2, c3 = (math.cos(math.pi * n / 8) for n in (1, 2, 3))
    s = [x[a] + x[a + 8] for a in range(8)]
    d = [x[a] - x[a + 8] for a in range(8)]
    ss = [s[a] + s[a + 4] for a in range(4)]
    sd = [s[a] - s[a + 4] for a in range(4)]
    p0, p1 = ss[0] + ss[2], ss[1] + ss[3]
    t1, t2 = c2 * (sd[1] - sd[3]), c2 * (sd[1] + sd[3])
    f = [None] + [d[a] - d[8 - a] for a in (1, 2, 3)]
    g = [None] + [d[a] + d[8 - a] for a in (1, 2, 3)]
    cf, cg = c2 * f[2], c2 * g[2]
    even, odd = d[0] + cf, d[0] - cf
    pp, qq = c1 * f[1] + c3 * f[3], c3 * f[1] - c1 * f[3]
    vv, ww = c3 * g[1] + c1 * g[3], c1 * g[1] - c3 * g[3]
    ee, ff = cg + d[4], cg - d[4]
    return [
        (p0 + p1, p0 - p1),
        (even + pp, -(vv + ee)),
        (sd[0] + t1, -(sd[2] + t2)),
        (odd + qq, -(ww + ff)),
        (ss[0] - ss[2], ss[3] - ss[1]),
        (odd - qq, ff - ww),
        (sd[0] - t1, sd[2] - t2),
        (even - pp, ee - vv),
    ]


def dot(left, right):
    return jnp.dot(left, right, preferred_element_type=F32)


def kernel(
    peers,
    blocks,
    samples,
    cell_in,
    window_in,
    channel_in,
    position_in,
    arrived,
    scale_in,
    frames,
    cell,
    window,
    channel,
    position,
    terms,
    outgoing,
    spectra,
    choose,
    along,
    energy,
    packed,
    scale_out,
    load_sem,
    halo_send,
    halo_recv,
    spectra_send,
    spectra_recv,
    power_send,
    power_recv,
    scale_send,
    scale_recv,
    around,
):
    me = lax.axis_index("chan")
    block = lax.axis_index("tm")
    is_first, is_last = block == 0, block == blocks - 1

    def device(flip, dy):
        return lax.rem(me // 8 + flip, 2) * 8 + lax.rem(lax.rem(me, 8) + 8 + dy, 8)

    def near(k):
        place = lax.rem(k + 2, 10)
        return device(place // 5, lax.rem(place, 5) - 2)

    def far(k):
        return device(k // 3, lax.rem(k, 3) + 3)

    def drained(ref, sem):
        pltpu.make_async_copy(ref, ref, sem).wait()

    barrier = pltpu.get_barrier_semaphore()

    @pl.when(jnp.logical_not(is_first))
    def _():
        pl.semaphore_signal(barrier, inc=1, device_id={"tm": block - 1}, device_id_type=MESH)

    def greet(k, carry):
        pl.semaphore_signal(barrier, inc=1, device_id={"chan": near(k)}, device_id_type=MESH)
        return carry

    lax.fori_loop(1, 10, greet, 0)

    for q in range(TSUM):
        pltpu.make_async_copy(
            samples.at[:, pl.ds(q * NFFT, NFFT)], frames.at[HISTORY + q], load_sem.at[0]
        ).start()
    loads = [
        pltpu.make_async_copy(source, target, load_sem.at[n + 1])
        for n, (source, target) in enumerate(
            ((window_in, window), (channel_in, channel), (position_in, position), (cell_in, cell))
        )
    ]
    for load in loads:
        load.start()

    def halo(f):
        return pltpu.make_async_remote_copy(
            src_ref=samples.at[:, pl.ds((f + 1) * NFFT, NFFT)],
            dst_ref=frames.at[f],
            send_sem=halo_send,
            recv_sem=halo_recv.at[f],
            device_id={"tm": block + 1},
            device_id_type=MESH,
        )

    def spectra_copy(t, target):
        return pltpu.make_async_remote_copy(
            src_ref=outgoing.at[t, target],
            dst_ref=spectra.at[t, me],
            send_sem=spectra_send,
            recv_sem=spectra_recv.at[t],
            device_id={"chan": target},
            device_id_type=MESH,
        )

    def power_copy(target):
        return pltpu.make_async_remote_copy(
            src_ref=packed.at[target],
            dst_ref=arrived.at[me],
            send_sem=power_send,
            recv_sem=power_recv,
            device_id={"chan": target},
            device_id_type=MESH,
        )

    def scale_copy(target):
        return pltpu.make_async_remote_copy(
            src_ref=scale_out.at[target],
            dst_ref=scale_in.at[me],
            send_sem=scale_send,
            recv_sem=scale_recv,
            device_id={"chan": target},
            device_id_type=MESH,
        )

    def filter_frame(t):
        def rows_of(r, carry):
            rows = pl.ds(pl.multiple_of(r * 16, 16), 16)
            x = []
            for a in range(STEP):
                lanes = pl.ds(a * FINE, FINE)
                total = None
                for k in range(TAPS):
                    term = window[pl.ds(k, 1), lanes] * frames[t + k, rows, lanes].astype(F32)
                    total = term if total is None else total + term
                x.append(total)
            for p, pair in enumerate(short_dft(x)):
                for part, value in enumerate(pair):
                    lanes = pl.ds(part * FINE, FINE)
                    high = value.astype(BF16)
                    terms[p, rows, lanes] = high
                    terms[p, pl.ds(pl.multiple_of(64 + r * 16, 16), 16), lanes] = (value - high.astype(F32)).astype(BF16)
            return carry

        lax.fori_loop(0, 4, rows_of, 0)

    def channelize(t):
        for p in range(STEP // 2):
            first = dot(terms[p], channel[0, p])
            second = dot(terms[p, pl.ds(0, 64), :], channel[1, p])
            result = (first[:64] + first[64:] + second).astype(BF16)
            outgoing[t, p] = result[:, :FINE]
            outgoing[t, 8 if p == 0 else STEP - p] = result[:, FINE:]

    def send_near(t):
        def one(k, carry):
            spectra_copy(t, near(k)).start()
            return carry

        lax.fori_loop(1, 10, one, 0)

    def send_far(t):
        def one(k, carry):
            spectra_copy(t, far(k)).start()
            return carry

        lax.fori_loop(0, 6, one, 0)
        spectra[t, me] = outgoing[t, me]

    drained(frames.at[pl.ds(HISTORY, TSUM)], load_sem.at[0])
    loads[0].wait()
    filter_frame(TSUM - 1)
    loads[1].wait()
    channelize(TSUM - 1)
    pl.semaphore_wait(barrier, jnp.where(is_last, 9, 10))
    for dy in (2, 6):
        pl.semaphore_signal(around, inc=1, device_id={"chan": device(0, dy)}, device_id_type=MESH)

    @pl.when(jnp.logical_not(is_last))
    def _():
        for f in (2, 1, 0):
            halo(f).start()

    send_near(TSUM - 1)
    pl.semaphore_wait(around, 2)
    send_far(TSUM - 1)

    loads[3].wait()

    def choose_rows(r, carry):
        first = pl.multiple_of(r * 32, 32)
        base = first // POSN * POSN + lax.rem(first, POSN // 2) * 2 + lax.rem(first // (POSN // 2), 2)
        number = lax.broadcasted_iota(jnp.int32, (32, INPUTS), 0) * 2 + base
        choose[pl.ds(first, 32), :] = jnp.where(number == cell[...], 1.0, 0.0).astype(BF16)
        return carry

    lax.fori_loop(0, INPUTS // 32, choose_rows, 0)

    def later_frame(step, carry):
        t = TSUM - 1 - step

        @pl.when(jnp.logical_not(is_first))
        def _():
            halo(t).wait_recv()

        @pl.when(is_first)
        def _():
            frames[t] = jnp.zeros((64, NFFT), BF16)

        filter_frame(t)
        channelize(t)
        send_far(t)
        send_near(t)
        return carry

    lax.fori_loop(1, TSUM, later_frame, 0)

    loads[2].wait()
    lane = lax.broadcasted_iota(jnp.int32, (1, FINE), 1)
    left = lane < HALF
    sign = jnp.where(left, 1.0, -1.0)

    def turned(value):
        return pltpu.roll(value, HALF, 1) * sign

    def beams_of(group):
        for t in group:
            drained(spectra.at[t, pl.ds(0, peers - 1)], spectra_recv.at[t])
        received = jnp.concatenate([spectra[t].reshape(INPUTS, FINE) for t in group], axis=1)
        half = POSN // 2
        for g in range(CYL):
            placed = dot(choose[pl.ds(g * POSN, POSN), :], received)
            swapped = jnp.concatenate([turned(placed[:, n * FINE : (n + 1) * FINE]) for n in range(len(group))], axis=1)
            sums = []
            for odd in range(2):
                rows = slice(odd * half, (odd + 1) * half)
                both = jnp.concatenate([placed[rows], swapped[rows]], axis=0).astype(BF16)
                parts = dot(position[odd], both)
                sums.append(parts[:half] + parts[half:])
            along[g, :half, : len(group) * FINE] = sums[0] + sums[1]
            along[g, half:, : len(group) * FINE] = sums[0] - sums[1]

    def power_of(group, first):
        def power_rows(r, carry):
            rows = pl.ds(pl.multiple_of(r * 32, 32), 32)
            squares = [None] * CYL
            for n in range(len(group)):
                a = [along[g, rows, pl.ds(n * FINE, FINE)] for g in range(CYL)]
                even, odd = a[0] + a[2], a[1] + a[3]
                across, quarter = a[0] - a[2], turned(a[1] - a[3])
                for u, beam in enumerate((even + odd, across + quarter, even - odd, across - quarter)):
                    squares[u] = beam * beam if n == 0 else squares[u] + beam * beam
            for duo in range(2):
                one, two = squares[2 * duo], squares[2 * duo + 1]
                folded = jnp.where(left, one, two) + pltpu.roll(jnp.where(left, two, one), HALF, 1)
                energy[duo, rows, :] = folded if first else energy[duo, rows, :] + folded
            return carry

        lax.fori_loop(0, POSN // 32, power_rows, 0, unroll=2)

    for n, group in enumerate(((3, 2), (1,), (0,))):
        beams_of(group)
        power_of(group, n == 0)

    largest = jnp.max(jnp.max(jnp.maximum(energy[0], energy[1]), axis=0, keepdims=True), axis=1, keepdims=True)
    largest = jnp.maximum(largest, 1e-36)
    scale_out[...] = jnp.broadcast_to((largest * (1.0 / (TSUM * INPUTS))).reshape(1, 1, 1), (peers, 1, 128))
    inverse = 1.0 / largest

    for duo in range(2):
        for side in range(2):
            share = energy[duo, pl.ds(side * 128, 128), :] * inverse
            share = share * share
            upright = (share * share).T
            for u in range(2):
                low = upright[u * HALF : u * HALF + 32]
                high = upright[u * HALF + 32 : u * HALF + 64]
                target = (2 * duo + u) * 4 + 2 * side
                packed[target] = jnp.where(left, low, pltpu.roll(high, HALF, 1)).astype(BF16)
                packed[target + 1] = jnp.where(left, pltpu.roll(low, HALF, 1), high).astype(BF16)

    def send_power(target):
        scale_copy(target).start()
        power_copy(target).start()

    def power_far(k, carry):
        send_power(far(k))
        return carry

    def power_near(k, carry):
        send_power(near(k))
        return carry

    lax.fori_loop(0, 6, power_far, 0)
    lax.fori_loop(1, 10, power_near, 0)
    arrived[me] = packed[me]
    scale_in[me] = scale_out[me]

    @pl.when(jnp.logical_not(is_last))
    def _():
        drained(frames.at[pl.ds(0, HISTORY)], halo_send)

    others = pl.ds(0, peers - 1)
    drained(outgoing.at[:, others], spectra_send)
    drained(packed.at[others], power_send)
    drained(scale_out.at[others], scale_send)
    drained(arrived.at[others], power_recv)
    drained(scale_in.at[others], scale_recv)


def interleave(arrived, scale, out, ordered):
    for s in range(STEP):
        ordered[pl.ds(s, 32, stride=STEP), :] = lax.rsqrt(lax.rsqrt(arrived[s].astype(F32))) * scale[s]
    for q in range(4):
        upright = ordered[pl.ds(q * 128, 128), :].T
        out[:, pl.ds(q * 128, 128)] = upright[:HALF]
        out[:, pl.ds(512 + q * 128, 128)] = upright[HALF:]


def local(peers, blocks, samples, cell_of_feed):
    vmem = pl.BlockSpec(memory_space=pltpu.VMEM)
    anywhere = pl.BlockSpec(memory_space=pl.ANY)
    dma = pltpu.SemaphoreType.DMA
    arrived, scale = pl.pallas_call(
        functools.partial(kernel, peers, blocks),
        out_shape=(
            pltpu.VMEM((peers, 32, 128), BF16),
            pltpu.VMEM((peers, 1, 128), F32),
        ),
        in_specs=[anywhere] * 5,
        out_specs=(vmem, vmem),
        scratch_shapes=[
            pltpu.VMEM((HISTORY + TSUM, 64, NFFT), BF16),
            pltpu.VMEM((1, INPUTS), jnp.int32),
            pltpu.VMEM((TAPS, NFFT), F32),
            pltpu.VMEM((2, STEP // 2, 2 * FINE, 2 * FINE), BF16),
            pltpu.VMEM((2, POSN, POSN), BF16),
            pltpu.VMEM((STEP // 2, 128, 2 * FINE), BF16),
            pltpu.VMEM((TSUM, peers, 64, FINE), BF16),
            pltpu.VMEM((TSUM, peers, 64, FINE), BF16),
            pltpu.VMEM((INPUTS, INPUTS), BF16),
            pltpu.VMEM((CYL, POSN, 2 * FINE), F32),
            pltpu.VMEM((2, POSN, FINE), F32),
            pltpu.VMEM((peers, 32, 128), BF16),
            pltpu.VMEM((peers, 1, 128), F32),
            dma((5,)),
            dma(()),
            dma((HISTORY,)),
            dma(()),
            dma((TSUM,)),
            dma(()),
            dma(()),
            dma(()),
            dma(()),
            pltpu.SemaphoreType.REGULAR,
        ],
        compiler_params=pltpu.CompilerParams(
            collective_id=0, has_side_effects=True, vmem_limit_bytes=60 * 1024 * 1024
        ),
    )(
        samples,
        cell_of_feed.reshape(1, INPUTS),
        jnp.asarray(window_table()),
        jnp.asarray(channel_tables()),
        jnp.asarray(position_tables()),
    )
    power = pl.pallas_call(
        interleave,
        out_shape=jax.ShapeDtypeStruct((64, 1024), F32),
        in_specs=[vmem, vmem],
        out_specs=vmem,
        scratch_shapes=[pltpu.VMEM((512, 128), F32)],
    )(arrived, scale)
    return power.reshape(1, 64, 1024)


def solution(mesh):
    return jax.shard_map(
        functools.partial(local, mesh.shape["chan"], mesh.shape["tm"]),
        mesh=mesh,
        in_specs=(P("chan", "tm"), P()),
        out_specs=P("tm", "chan", None),
        check_vma=False,
    )
```

```python
import functools
import math

import jax
import jax.numpy as jnp
import ml_dtypes
import numpy as np
from jax import lax
from jax.experimental import pallas as pl
from jax.experimental.pallas import tpu as pltpu
from jax.sharding import PartitionSpec as P

POSN = 256
CYL = 4
NFFT = 2048
TAPS = 4
TSUM = 4
INPUTS = 1024

STEP = 16
FINE = NFFT // STEP
HALF = FINE // 2
HISTORY = TAPS - 1

BF16 = jnp.bfloat16
F32 = jnp.float32
MESH = pl.DeviceIdType.MESH


def two_parts(table):
    high = table.astype(ml_dtypes.bfloat16)
    low = (table - high.astype(np.float64)).astype(ml_dtypes.bfloat16)
    return np.stack([high, low])


def window_table():
    offsets = np.arange(TAPS * NFFT) + 0.5
    shaped = np.sinc(offsets / NFFT - TAPS / 2.0)
    tapered = 0.5 - 0.5 * np.cos(offsets * (2.0 * math.pi / (TAPS * NFFT)))
    return (shaped * tapered).reshape(TAPS, NFFT).astype(np.float32)


def channel_tables():
    b = np.arange(FINE)[:, None]
    j = np.arange(HALF)[None, :]

    def waves(s):
        angle = 2.0 * math.pi * ((b * (STEP * j + s)) % NFFT) / NFFT
        return np.cos(angle), np.sin(angle)

    out = np.zeros((STEP // 2, 2 * FINE, 2 * FINE))
    for half, s in enumerate((0, STEP // 2)):
        cos, sin = waves(s)
        out[0, half * FINE : (half + 1) * FINE, half * FINE : (half + 1) * FINE] = np.concatenate([cos, -sin], 1)
    for p in range(1, STEP // 2):
        cos, sin = waves(p)
        out[p, :FINE, :FINE] = np.concatenate([cos, -sin], 1)
        out[p, FINE:, :FINE] = np.concatenate([sin, cos], 1)
        cos, sin = waves(STEP - p)
        out[p, :FINE, FINE:] = np.concatenate([cos, -sin], 1)
        out[p, FINE:, FINE:] = np.concatenate([-sin, -cos], 1)
    return two_parts(out / math.sqrt(NFFT))


def position_tables():
    v, r = np.arange(POSN // 2)[:, None], np.arange(POSN // 2)[None, :]
    out = []
    for odd in range(2):
        angle = 2.0 * math.pi * ((v * (2 * r + odd)) % POSN) / POSN
        out.append(np.concatenate(two_parts(np.concatenate([np.cos(angle), np.sin(angle)], 1))))
    return np.stack(out)


def short_dft(x):
    c1, c2, c3 = (math.cos(math.pi * n / 8) for n in (1, 2, 3))
    s = [x[a] + x[a + 8] for a in range(8)]
    d = [x[a] - x[a + 8] for a in range(8)]
    ss = [s[a] + s[a + 4] for a in range(4)]
    sd = [s[a] - s[a + 4] for a in range(4)]
    p0, p1 = ss[0] + ss[2], ss[1] + ss[3]
    t1, t2 = c2 * (sd[1] - sd[3]), c2 * (sd[1] + sd[3])
    f = [None] + [d[a] - d[8 - a] for a in (1, 2, 3)]
    g = [None] + [d[a] + d[8 - a] for a in (1, 2, 3)]
    cf, cg = c2 * f[2], c2 * g[2]
    even, odd = d[0] + cf, d[0] - cf
    pp, qq = c1 * f[1] + c3 * f[3], c3 * f[1] - c1 * f[3]
    vv, ww = c3 * g[1] + c1 * g[3], c1 * g[1] - c3 * g[3]
    ee, ff = cg + d[4], cg - d[4]
    return [
        (p0 + p1, p0 - p1),
        (even + pp, -(vv + ee)),
        (sd[0] + t1, -(sd[2] + t2)),
        (odd + qq, -(ww + ff)),
        (ss[0] - ss[2], ss[3] - ss[1]),
        (odd - qq, ff - ww),
        (sd[0] - t1, sd[2] - t2),
        (even - pp, ee - vv),
    ]


def dot(left, right):
    return jnp.dot(left, right, preferred_element_type=F32)


def kernel(
    peers,
    blocks,
    samples,
    cell_in,
    window_in,
    channel_in,
    position_in,
    arrived,
    scale_in,
    frames,
    cell,
    window,
    channel,
    position,
    terms,
    outgoing,
    spectra,
    choose,
    along,
    energy,
    packed,
    scale_out,
    load_sem,
    halo_send,
    halo_recv,
    spectra_send,
    spectra_recv,
    power_send,
    power_recv,
    scale_send,
    scale_recv,
    around,
):
    me = lax.axis_index("chan")
    block = lax.axis_index("tm")
    is_first, is_last = block == 0, block == blocks - 1

    def device(flip, dy):
        return lax.rem(me // 8 + flip, 2) * 8 + lax.rem(lax.rem(me, 8) + 8 + dy, 8)

    def near(k):
        place = lax.rem(k + 2, 10)
        return device(place // 5, lax.rem(place, 5) - 2)

    def far(k):
        return device(k // 3, lax.rem(k, 3) + 3)

    def drained(ref, sem):
        pltpu.make_async_copy(ref, ref, sem).wait()

    barrier = pltpu.get_barrier_semaphore()

    @pl.when(jnp.logical_not(is_first))
    def _():
        pl.semaphore_signal(barrier, inc=1, device_id={"tm": block - 1}, device_id_type=MESH)

    def greet(k, carry):
        pl.semaphore_signal(barrier, inc=1, device_id={"chan": near(k)}, device_id_type=MESH)
        return carry

    lax.fori_loop(1, 10, greet, 0)

    for q in range(TSUM):
        pltpu.make_async_copy(
            samples.at[:, pl.ds(q * NFFT, NFFT)], frames.at[HISTORY + q], load_sem.at[0]
        ).start()
    loads = [
        pltpu.make_async_copy(source, target, load_sem.at[n + 1])
        for n, (source, target) in enumerate(
            ((window_in, window), (channel_in, channel), (position_in, position), (cell_in, cell))
        )
    ]
    for load in loads:
        load.start()

    def halo(f):
        return pltpu.make_async_remote_copy(
            src_ref=samples.at[:, pl.ds((f + 1) * NFFT, NFFT)],
            dst_ref=frames.at[f],
            send_sem=halo_send,
            recv_sem=halo_recv.at[f],
            device_id={"tm": block + 1},
            device_id_type=MESH,
        )

    def spectra_copy(t, target):
        return pltpu.make_async_remote_copy(
            src_ref=outgoing.at[t, target],
            dst_ref=spectra.at[t, me],
            send_sem=spectra_send,
            recv_sem=spectra_recv.at[t],
            device_id={"chan": target},
            device_id_type=MESH,
        )

    def power_copy(target):
        return pltpu.make_async_remote_copy(
            src_ref=packed.at[target],
            dst_ref=arrived.at[me],
            send_sem=power_send,
            recv_sem=power_recv,
            device_id={"chan": target},
            device_id_type=MESH,
        )

    def scale_copy(target):
        return pltpu.make_async_remote_copy(
            src_ref=scale_out.at[target],
            dst_ref=scale_in.at[me],
            send_sem=scale_send,
            recv_sem=scale_recv,
            device_id={"chan": target},
            device_id_type=MESH,
        )

    def filter_frame(t):
        def rows_of(r, carry):
            rows = pl.ds(pl.multiple_of(r * 16, 16), 16)
            x = []
            for a in range(STEP):
                lanes = pl.ds(a * FINE, FINE)
                total = None
                for k in range(TAPS):
                    term = window[pl.ds(k, 1), lanes] * frames[t + k, rows, lanes].astype(F32)
                    total = term if total is None else total + term
                x.append(total)
            for p, pair in enumerate(short_dft(x)):
                for part, value in enumerate(pair):
                    lanes = pl.ds(part * FINE, FINE)
                    high = value.astype(BF16)
                    terms[p, rows, lanes] = high
                    terms[p, pl.ds(pl.multiple_of(64 + r * 16, 16), 16), lanes] = (value - high.astype(F32)).astype(BF16)
            return carry

        lax.fori_loop(0, 4, rows_of, 0)

    def channelize(t):
        for p in range(STEP // 2):
            first = dot(terms[p], channel[0, p])
            second = dot(terms[p, pl.ds(0, 64), :], channel[1, p])
            result = (first[:64] + first[64:] + second).astype(BF16)
            outgoing[t, p] = result[:, :FINE]
            outgoing[t, 8 if p == 0 else STEP - p] = result[:, FINE:]

    def send_near(t):
        def one(k, carry):
            spectra_copy(t, near(k)).start()
            return carry

        lax.fori_loop(1, 10, one, 0)

    def send_far(t):
        def one(k, carry):
            spectra_copy(t, far(k)).start()
            return carry

        lax.fori_loop(0, 6, one, 0)
        spectra[t, me] = outgoing[t, me]

    drained(frames.at[pl.ds(HISTORY, TSUM)], load_sem.at[0])
    loads[0].wait()
    filter_frame(TSUM - 1)
    loads[1].wait()
    channelize(TSUM - 1)
    pl.semaphore_wait(barrier, jnp.where(is_last, 9, 10))
    for dy in (2, 6):
        pl.semaphore_signal(around, inc=1, device_id={"chan": device(0, dy)}, device_id_type=MESH)

    @pl.when(jnp.logical_not(is_last))
    def _():
        for f in (2, 1, 0):
            halo(f).start()

    send_near(TSUM - 1)
    pl.semaphore_wait(around, 2)
    send_far(TSUM - 1)

    loads[3].wait()

    def choose_rows(r, carry):
        first = pl.multiple_of(r * 32, 32)
        base = first // POSN * POSN + lax.rem(first, POSN // 2) * 2 + lax.rem(first // (POSN // 2), 2)
        number = lax.broadcasted_iota(jnp.int32, (32, INPUTS), 0) * 2 + base
        choose[pl.ds(first, 32), :] = jnp.where(number == cell[...], 1.0, 0.0).astype(BF16)
        return carry

    lax.fori_loop(0, INPUTS // 32, choose_rows, 0)

    def later_frame(step, carry):
        t = TSUM - 1 - step

        @pl.when(jnp.logical_not(is_first))
        def _():
            halo(t).wait_recv()

        @pl.when(is_first)
        def _():
            frames[t] = jnp.zeros((64, NFFT), BF16)

        filter_frame(t)
        channelize(t)
        send_far(t)
        send_near(t)
        return carry

    lax.fori_loop(1, TSUM, later_frame, 0)

    loads[2].wait()
    lane = lax.broadcasted_iota(jnp.int32, (1, FINE), 1)
    left = lane < HALF
    sign = jnp.where(left, 1.0, -1.0)

    def turned(value):
        return pltpu.roll(value, HALF, 1) * sign

    def beams_of(group):
        for t in group:
            drained(spectra.at[t, pl.ds(0, peers - 1)], spectra_recv.at[t])
        received = jnp.concatenate([spectra[t].reshape(INPUTS, FINE) for t in group], axis=1)
        half = POSN // 2
        for g in range(CYL):
            placed = dot(choose[pl.ds(g * POSN, POSN), :], received)
            swapped = jnp.concatenate([turned(placed[:, n * FINE : (n + 1) * FINE]) for n in range(len(group))], axis=1)
            sums = []
            for odd in range(2):
                rows = slice(odd * half, (odd + 1) * half)
                both = jnp.concatenate([placed[rows], swapped[rows]], axis=0).astype(BF16)
                parts = dot(position[odd], both)
                sums.append(parts[:half] + parts[half:])
            along[g, :half, : len(group) * FINE] = sums[0] + sums[1]
            along[g, half:, : len(group) * FINE] = sums[0] - sums[1]

    def power_of(group, first):
        def power_rows(r, carry):
            rows = pl.ds(pl.multiple_of(r * 32, 32), 32)
            squares = [None] * CYL
            for n in range(len(group)):
                a = [along[g, rows, pl.ds(n * FINE, FINE)] for g in range(CYL)]
                even, odd = a[0] + a[2], a[1] + a[3]
                across, quarter = a[0] - a[2], turned(a[1] - a[3])
                for u, beam in enumerate((even + odd, across + quarter, even - odd, across - quarter)):
                    squares[u] = beam * beam if n == 0 else squares[u] + beam * beam
            for duo in range(2):
                one, two = squares[2 * duo], squares[2 * duo + 1]
                folded = jnp.where(left, one, two) + pltpu.roll(jnp.where(left, two, one), HALF, 1)
                folded = folded if first else energy[duo, rows, :] + folded
                energy[duo, rows, :] = folded
                carry = jnp.maximum(carry, jnp.max(folded.reshape(-1, 8, FINE), axis=0))
            return carry

        return lax.fori_loop(0, POSN // 32, power_rows, jnp.zeros((8, FINE), F32), unroll=4)

    for n, group in enumerate(((3, 2), (1,), (0,))):
        beams_of(group)
        heights = power_of(group, n == 0)

    largest = jnp.max(jnp.max(heights, axis=0, keepdims=True), axis=1, keepdims=True)
    largest = jnp.maximum(largest, 1e-36)
    scale_out[...] = jnp.broadcast_to((largest * (1.0 / (TSUM * INPUTS))).reshape(1, 1, 1), (peers, 1, 128))
    inverse = 1.0 / largest

    for duo in range(2):
        for side in range(2):
            share = energy[duo, pl.ds(side * 128, 128), :] * inverse
            share = share * share
            upright = (share * share).T
            for u in range(2):
                low = upright[u * HALF : u * HALF + 32]
                high = upright[u * HALF + 32 : u * HALF + 64]
                target = (2 * duo + u) * 4 + 2 * side
                packed[target] = jnp.where(left, low, pltpu.roll(high, HALF, 1)).astype(BF16)
                packed[target + 1] = jnp.where(left, pltpu.roll(low, HALF, 1), high).astype(BF16)

    def send_power(which, first, last):
        def blocks_of(k, carry):
            power_copy(which(k)).start()
            return carry

        def scales_of(k, carry):
            scale_copy(which(k)).start()
            return carry

        lax.fori_loop(first, last, blocks_of, 0)
        lax.fori_loop(first, last, scales_of, 0)

    send_power(far, 0, 6)
    send_power(near, 1, 10)
    arrived[me] = packed[me]
    scale_in[me] = scale_out[me]

    @pl.when(jnp.logical_not(is_last))
    def _():
        drained(frames.at[pl.ds(0, HISTORY)], halo_send)

    others = pl.ds(0, peers - 1)
    drained(outgoing.at[:, others], spectra_send)
    drained(packed.at[others], power_send)
    drained(scale_out.at[others], scale_send)
    drained(arrived.at[others], power_recv)
    drained(scale_in.at[others], scale_recv)


def interleave(arrived, scale, out, ordered, ready, sem):
    copies = []
    for q in range(4):
        for s in range(STEP):
            value = arrived[s, pl.ds(8 * q, 8), :].astype(F32)
            ordered[pl.ds(q * 128 + s, 8, stride=STEP), :] = lax.rsqrt(lax.rsqrt(value)) * scale[s]
        upright = ordered[pl.ds(q * 128, 128), :].T
        for high in range(2):
            lanes = pl.ds(512 * high + 128 * q, 128)
            ready[:, lanes] = upright[HALF * high : HALF * (high + 1)]
            copies.append(pltpu.make_async_copy(ready.at[:, lanes], out.at[:, lanes], sem.at[2 * q + high]))
            copies[-1].start()
    for copy in copies:
        copy.wait()


def local(peers, blocks, samples, cell_of_feed):
    vmem = pl.BlockSpec(memory_space=pltpu.VMEM)
    anywhere = pl.BlockSpec(memory_space=pl.ANY)
    dma = pltpu.SemaphoreType.DMA
    arrived, scale = pl.pallas_call(
        functools.partial(kernel, peers, blocks),
        out_shape=(
            pltpu.VMEM((peers, 32, 128), BF16),
            pltpu.VMEM((peers, 1, 128), F32),
        ),
        in_specs=[anywhere] * 5,
        out_specs=(vmem, vmem),
        scratch_shapes=[
            pltpu.VMEM((HISTORY + TSUM, 64, NFFT), BF16),
            pltpu.VMEM((1, INPUTS), jnp.int32),
            pltpu.VMEM((TAPS, NFFT), F32),
            pltpu.VMEM((2, STEP // 2, 2 * FINE, 2 * FINE), BF16),
            pltpu.VMEM((2, POSN, POSN), BF16),
            pltpu.VMEM((STEP // 2, 128, 2 * FINE), BF16),
            pltpu.VMEM((TSUM, peers, 64, FINE), BF16),
            pltpu.VMEM((TSUM, peers, 64, FINE), BF16),
            pltpu.VMEM((INPUTS, INPUTS), BF16),
            pltpu.VMEM((CYL, POSN, 2 * FINE), F32),
            pltpu.VMEM((2, POSN, FINE), F32),
            pltpu.VMEM((peers, 32, 128), BF16),
            pltpu.VMEM((peers, 1, 128), F32),
            dma((5,)),
            dma(()),
            dma((HISTORY,)),
            dma(()),
            dma((TSUM,)),
            dma(()),
            dma(()),
            dma(()),
            dma(()),
            pltpu.SemaphoreType.REGULAR,
        ],
        compiler_params=pltpu.CompilerParams(
            collective_id=0, has_side_effects=True, vmem_limit_bytes=60 * 1024 * 1024
        ),
    )(
        samples,
        cell_of_feed.reshape(1, INPUTS),
        jnp.asarray(window_table()),
        jnp.asarray(channel_tables()),
        jnp.asarray(position_tables()),
    )
    power = pl.pallas_call(
        interleave,
        out_shape=jax.ShapeDtypeStruct((64, 1024), F32),
        in_specs=[vmem, vmem],
        out_specs=anywhere,
        scratch_shapes=[pltpu.VMEM((512, 128), F32), pltpu.VMEM((64, 1024), F32), dma((8,))],
        compiler_params=pltpu.CompilerParams(vmem_limit_bytes=8 * 1024 * 1024),
    )(arrived, scale)
    return power.reshape(1, 64, 1024)


def solution(mesh):
    return jax.shard_map(
        functools.partial(local, mesh.shape["chan"], mesh.shape["tm"]),
        mesh=mesh,
        in_specs=(P("chan", "tm"), P()),
        out_specs=P("tm", "chan", None),
        check_vma=False,
    )
```

```python
import functools
import math

import jax
import jax.numpy as jnp
import ml_dtypes
import numpy as np
from jax import lax
from jax.experimental import pallas as pl
from jax.experimental.pallas import tpu as pltpu
from jax.sharding import PartitionSpec as P

POSN = 256
CYL = 4
NFFT = 2048
TAPS = 4
TSUM = 4
INPUTS = 1024

STEP = 16
FINE = NFFT // STEP
HALF = FINE // 2
HISTORY = TAPS - 1

BF16 = jnp.bfloat16
F32 = jnp.float32
MESH = pl.DeviceIdType.MESH


def two_parts(table):
    high = table.astype(ml_dtypes.bfloat16)
    low = (table - high.astype(np.float64)).astype(ml_dtypes.bfloat16)
    return np.stack([high, low])


def window_table():
    offsets = np.arange(TAPS * NFFT) + 0.5
    shaped = np.sinc(offsets / NFFT - TAPS / 2.0)
    tapered = 0.5 - 0.5 * np.cos(offsets * (2.0 * math.pi / (TAPS * NFFT)))
    return (shaped * tapered).reshape(TAPS, NFFT).astype(np.float32)


def channel_tables():
    b = np.arange(FINE)[:, None]
    j = np.arange(HALF)[None, :]

    def waves(s):
        angle = 2.0 * math.pi * ((b * (STEP * j + s)) % NFFT) / NFFT
        return np.cos(angle), np.sin(angle)

    out = np.zeros((STEP // 2, 2 * FINE, 2 * FINE))
    for half, s in enumerate((0, STEP // 2)):
        cos, sin = waves(s)
        out[0, half * FINE : (half + 1) * FINE, half * FINE : (half + 1) * FINE] = np.concatenate([cos, -sin], 1)
    for p in range(1, STEP // 2):
        cos, sin = waves(p)
        out[p, :FINE, :FINE] = np.concatenate([cos, -sin], 1)
        out[p, FINE:, :FINE] = np.concatenate([sin, cos], 1)
        cos, sin = waves(STEP - p)
        out[p, :FINE, FINE:] = np.concatenate([cos, -sin], 1)
        out[p, FINE:, FINE:] = np.concatenate([-sin, -cos], 1)
    return two_parts(out / math.sqrt(NFFT))


def position_tables():
    v, r = np.arange(POSN // 2)[:, None], np.arange(POSN // 2)[None, :]
    out = []
    for odd in range(2):
        angle = 2.0 * math.pi * ((v * (2 * r + odd)) % POSN) / POSN
        out.append(np.concatenate(two_parts(np.concatenate([np.cos(angle), np.sin(angle)], 1))))
    return np.stack(out)


def short_dft(x):
    c1, c2, c3 = (math.cos(math.pi * n / 8) for n in (1, 2, 3))
    s = [x[a] + x[a + 8] for a in range(8)]
    d = [x[a] - x[a + 8] for a in range(8)]
    ss = [s[a] + s[a + 4] for a in range(4)]
    sd = [s[a] - s[a + 4] for a in range(4)]
    p0, p1 = ss[0] + ss[2], ss[1] + ss[3]
    t1, t2 = c2 * (sd[1] - sd[3]), c2 * (sd[1] + sd[3])
    f = [None] + [d[a] - d[8 - a] for a in (1, 2, 3)]
    g = [None] + [d[a] + d[8 - a] for a in (1, 2, 3)]
    cf, cg = c2 * f[2], c2 * g[2]
    even, odd = d[0] + cf, d[0] - cf
    pp, qq = c1 * f[1] + c3 * f[3], c3 * f[1] - c1 * f[3]
    vv, ww = c3 * g[1] + c1 * g[3], c1 * g[1] - c3 * g[3]
    ee, ff = cg + d[4], cg - d[4]
    return [
        (p0 + p1, p0 - p1),
        (even + pp, -(vv + ee)),
        (sd[0] + t1, -(sd[2] + t2)),
        (odd + qq, -(ww + ff)),
        (ss[0] - ss[2], ss[3] - ss[1]),
        (odd - qq, ff - ww),
        (sd[0] - t1, sd[2] - t2),
        (even - pp, ee - vv),
    ]


def dot(left, right):
    return jnp.dot(left, right, preferred_element_type=F32)


def kernel(
    peers,
    blocks,
    samples,
    cell_in,
    window_in,
    channel_in,
    position_in,
    arrived,
    scale_in,
    frames,
    cell,
    window,
    channel,
    position,
    terms,
    outgoing,
    spectra,
    choose,
    along,
    energy,
    packed,
    scale_out,
    load_sem,
    halo_send,
    halo_recv,
    spectra_send,
    spectra_recv,
    power_send,
    power_recv,
    scale_send,
    scale_recv,
    around,
):
    me = lax.axis_index("chan")
    block = lax.axis_index("tm")
    is_first, is_last = block == 0, block == blocks - 1

    def device(flip, dy):
        return lax.rem(me // 8 + flip, 2) * 8 + lax.rem(lax.rem(me, 8) + 8 + dy, 8)

    def near(k):
        place = lax.rem(k + 2, 10)
        return device(place // 5, lax.rem(place, 5) - 2)

    def far(k):
        return device(k // 3, lax.rem(k, 3) + 3)

    def drained(ref, sem):
        pltpu.make_async_copy(ref, ref, sem).wait()

    barrier = pltpu.get_barrier_semaphore()

    @pl.when(jnp.logical_not(is_first))
    def _():
        pl.semaphore_signal(barrier, inc=1, device_id={"tm": block - 1}, device_id_type=MESH)

    def greet(k, carry):
        pl.semaphore_signal(barrier, inc=1, device_id={"chan": near(k)}, device_id_type=MESH)
        return carry

    lax.fori_loop(1, 10, greet, 0)

    for q in range(TSUM):
        pltpu.make_async_copy(
            samples.at[:, pl.ds(q * NFFT, NFFT)], frames.at[HISTORY + q], load_sem.at[0]
        ).start()
    loads = [
        pltpu.make_async_copy(source, target, load_sem.at[n + 1])
        for n, (source, target) in enumerate(
            ((window_in, window), (channel_in, channel), (position_in, position), (cell_in, cell))
        )
    ]
    for load in loads:
        load.start()

    def halo(f):
        return pltpu.make_async_remote_copy(
            src_ref=samples.at[:, pl.ds((f + 1) * NFFT, NFFT)],
            dst_ref=frames.at[f],
            send_sem=halo_send,
            recv_sem=halo_recv.at[f],
            device_id={"tm": block + 1},
            device_id_type=MESH,
        )

    def spectra_copy(t, target):
        return pltpu.make_async_remote_copy(
            src_ref=outgoing.at[t, target],
            dst_ref=spectra.at[t, me],
            send_sem=spectra_send,
            recv_sem=spectra_recv.at[t],
            device_id={"chan": target},
            device_id_type=MESH,
        )

    def power_copy(target):
        return pltpu.make_async_remote_copy(
            src_ref=packed.at[target],
            dst_ref=arrived.at[me],
            send_sem=power_send,
            recv_sem=power_recv,
            device_id={"chan": target},
            device_id_type=MESH,
        )

    def scale_copy(target):
        return pltpu.make_async_remote_copy(
            src_ref=scale_out.at[target],
            dst_ref=scale_in.at[me],
            send_sem=scale_send,
            recv_sem=scale_recv,
            device_id={"chan": target},
            device_id_type=MESH,
        )

    def filter_frame(t):
        def rows_of(r, carry):
            rows = pl.ds(pl.multiple_of(r * 16, 16), 16)
            x = []
            for a in range(STEP):
                lanes = pl.ds(a * FINE, FINE)
                total = None
                for k in range(TAPS):
                    term = window[pl.ds(k, 1), lanes] * frames[t + k, rows, lanes].astype(F32)
                    total = term if total is None else total + term
                x.append(total)
            for p, pair in enumerate(short_dft(x)):
                for part, value in enumerate(pair):
                    lanes = pl.ds(part * FINE, FINE)
                    high = value.astype(BF16)
                    terms[p, rows, lanes] = high
                    terms[p, pl.ds(pl.multiple_of(64 + r * 16, 16), 16), lanes] = (value - high.astype(F32)).astype(BF16)
            return carry

        lax.fori_loop(0, 4, rows_of, 0)

    def channelize(t):
        for p in range(STEP // 2):
            first = dot(terms[p], channel[0, p])
            second = dot(terms[p, pl.ds(0, 64), :], channel[1, p])
            result = (first[:64] + first[64:] + second).astype(BF16)
            outgoing[t, p] = result[:, :FINE]
            outgoing[t, 8 if p == 0 else STEP - p] = result[:, FINE:]

    def send_near(t):
        def one(k, carry):
            spectra_copy(t, near(k)).start()
            return carry

        lax.fori_loop(1, 10, one, 0)

    def send_far(t):
        def one(k, carry):
            spectra_copy(t, far(k)).start()
            return carry

        lax.fori_loop(0, 6, one, 0)
        spectra[t, me] = outgoing[t, me]

    drained(frames.at[pl.ds(HISTORY, TSUM)], load_sem.at[0])
    loads[0].wait()
    filter_frame(TSUM - 1)
    loads[1].wait()
    channelize(TSUM - 1)
    pl.semaphore_wait(barrier, jnp.where(is_last, 9, 10))
    for dy in (2, 6):
        pl.semaphore_signal(around, inc=1, device_id={"chan": device(0, dy)}, device_id_type=MESH)

    @pl.when(jnp.logical_not(is_last))
    def _():
        for f in (2, 1, 0):
            halo(f).start()

    send_near(TSUM - 1)
    pl.semaphore_wait(around, 2)
    send_far(TSUM - 1)

    loads[3].wait()

    def choose_rows(r, carry):
        first = pl.multiple_of(r * 32, 32)
        base = first // POSN * POSN + lax.rem(first, POSN // 2) * 2 + lax.rem(first // (POSN // 2), 2)
        number = lax.broadcasted_iota(jnp.int32, (32, INPUTS), 0) * 2 + base
        choose[pl.ds(first, 32), :] = jnp.where(number == cell[...], 1.0, 0.0).astype(BF16)
        return carry

    lax.fori_loop(0, INPUTS // 32, choose_rows, 0)

    def later_frame(step, carry):
        t = TSUM - 1 - step

        @pl.when(jnp.logical_not(is_first))
        def _():
            halo(t).wait_recv()

        @pl.when(is_first)
        def _():
            frames[t] = jnp.zeros((64, NFFT), BF16)

        filter_frame(t)
        channelize(t)
        send_far(t)
        send_near(t)
        return carry

    lax.fori_loop(1, TSUM, later_frame, 0)

    loads[2].wait()
    lane = lax.broadcasted_iota(jnp.int32, (1, FINE), 1)
    left = lane < HALF
    sign = jnp.where(left, 1.0, -1.0)

    def turned(value):
        return pltpu.roll(value, HALF, 1) * sign

    def beams_of(group):
        for t in group:
            drained(spectra.at[t, pl.ds(0, peers - 1)], spectra_recv.at[t])
        received = jnp.concatenate([spectra[t].reshape(INPUTS, FINE) for t in group], axis=1)
        half = POSN // 2
        for g in range(CYL):
            placed = dot(choose[pl.ds(g * POSN, POSN), :], received)
            swapped = jnp.concatenate([turned(placed[:, n * FINE : (n + 1) * FINE]) for n in range(len(group))], axis=1)
            sums = []
            for odd in range(2):
                rows = slice(odd * half, (odd + 1) * half)
                both = jnp.concatenate([placed[rows], swapped[rows]], axis=0).astype(BF16)
                parts = dot(position[odd], both)
                sums.append(parts[:half] + parts[half:])
            along[g, :half, : len(group) * FINE] = sums[0] + sums[1]
            along[g, half:, : len(group) * FINE] = sums[0] - sums[1]

    def power_of(group, first):
        def power_rows(r, carry):
            rows = pl.ds(pl.multiple_of(r * 32, 32), 32)
            squares = [None] * CYL
            for n in range(len(group)):
                a = [along[g, rows, pl.ds(n * FINE, FINE)] for g in range(CYL)]
                even, odd = a[0] + a[2], a[1] + a[3]
                across, quarter = a[0] - a[2], turned(a[1] - a[3])
                for u, beam in enumerate((even + odd, across + quarter, even - odd, across - quarter)):
                    squares[u] = beam * beam if n == 0 else squares[u] + beam * beam
            for duo in range(2):
                one, two = squares[2 * duo], squares[2 * duo + 1]
                folded = jnp.where(left, one, two) + pltpu.roll(jnp.where(left, two, one), HALF, 1)
                folded = folded if first else energy[duo, rows, :] + folded
                energy[duo, rows, :] = folded
                carry = jnp.maximum(carry, jnp.max(folded.reshape(-1, 8, FINE), axis=0))
            return carry

        return lax.fori_loop(0, POSN // 32, power_rows, jnp.zeros((8, FINE), F32), unroll=4)

    for n, group in enumerate(((3, 2), (1,), (0,))):
        beams_of(group)
        heights = power_of(group, n == 0)

    largest = jnp.max(jnp.max(heights, axis=0, keepdims=True), axis=1, keepdims=True)
    largest = jnp.maximum(largest, 1e-36)
    scale_out[...] = jnp.broadcast_to((largest * (1.0 / (TSUM * INPUTS))).reshape(1, 1, 1), (peers, 1, 128))
    inverse = 1.0 / largest

    for duo in range(2):
        for side in range(2):
            share = energy[duo, pl.ds(side * 128, 128), :] * inverse
            share = share * share
            upright = (share * share).T
            for u in range(2):
                low = upright[u * HALF : u * HALF + 32]
                high = upright[u * HALF + 32 : u * HALF + 64]
                target = (2 * duo + u) * 4 + 2 * side
                packed[target] = jnp.where(left, low, pltpu.roll(high, HALF, 1)).astype(BF16)
                packed[target + 1] = jnp.where(left, pltpu.roll(low, HALF, 1), high).astype(BF16)

    def send_power(which, first, last):
        def blocks_of(k, carry):
            power_copy(which(k)).start()
            return carry

        def scales_of(k, carry):
            scale_copy(which(k)).start()
            return carry

        lax.fori_loop(first, last, blocks_of, 0)
        lax.fori_loop(first, last, scales_of, 0)

    send_power(far, 0, 6)
    send_power(near, 1, 10)
    arrived[me] = packed[me]
    scale_in[me] = scale_out[me]

    @pl.when(jnp.logical_not(is_last))
    def _():
        drained(frames.at[pl.ds(0, HISTORY)], halo_send)

    others = pl.ds(0, peers - 1)
    drained(outgoing.at[:, others], spectra_send)
    drained(packed.at[others], power_send)
    drained(scale_out.at[others], scale_send)
    drained(arrived.at[others], power_recv)
    drained(scale_in.at[others], scale_recv)


def interleave(arrived, scale, out, ordered, ready, sem):
    copies = []
    for q in range(4):
        for s in range(STEP if q % 2 == 0 else 0):
            value = arrived[s, pl.ds(8 * q, 16), :].astype(F32)
            ordered[pl.ds(q * 128 + s, 16, stride=STEP), :] = lax.rsqrt(lax.rsqrt(value)) * scale[s]
        upright = ordered[pl.ds(q * 128, 128), :].T
        for high in range(2):
            lanes = pl.ds(512 * high + 128 * q, 128)
            ready[:, lanes] = upright[HALF * high : HALF * (high + 1)]
            copies.append(pltpu.make_async_copy(ready.at[:, lanes], out.at[:, lanes], sem.at[2 * q + high]))
            copies[-1].start()
    for copy in copies:
        copy.wait()


def local(peers, blocks, samples, cell_of_feed):
    vmem = pl.BlockSpec(memory_space=pltpu.VMEM)
    anywhere = pl.BlockSpec(memory_space=pl.ANY)
    dma = pltpu.SemaphoreType.DMA
    arrived, scale = pl.pallas_call(
        functools.partial(kernel, peers, blocks),
        out_shape=(
            pltpu.VMEM((peers, 32, 128), BF16),
            pltpu.VMEM((peers, 1, 128), F32),
        ),
        in_specs=[anywhere] * 5,
        out_specs=(vmem, vmem),
        scratch_shapes=[
            pltpu.VMEM((HISTORY + TSUM, 64, NFFT), BF16),
            pltpu.VMEM((1, INPUTS), jnp.int32),
            pltpu.VMEM((TAPS, NFFT), F32),
            pltpu.VMEM((2, STEP // 2, 2 * FINE, 2 * FINE), BF16),
            pltpu.VMEM((2, POSN, POSN), BF16),
            pltpu.VMEM((STEP // 2, 128, 2 * FINE), BF16),
            pltpu.VMEM((TSUM, peers, 64, FINE), BF16),
            pltpu.VMEM((TSUM, peers, 64, FINE), BF16),
            pltpu.VMEM((INPUTS, INPUTS), BF16),
            pltpu.VMEM((CYL, POSN, 2 * FINE), F32),
            pltpu.VMEM((2, POSN, FINE), F32),
            pltpu.VMEM((peers, 32, 128), BF16),
            pltpu.VMEM((peers, 1, 128), F32),
            dma((5,)),
            dma(()),
            dma((HISTORY,)),
            dma(()),
            dma((TSUM,)),
            dma(()),
            dma(()),
            dma(()),
            dma(()),
            pltpu.SemaphoreType.REGULAR,
        ],
        compiler_params=pltpu.CompilerParams(
            collective_id=0, has_side_effects=True, vmem_limit_bytes=60 * 1024 * 1024
        ),
    )(
        samples,
        cell_of_feed.reshape(1, INPUTS),
        jnp.asarray(window_table()),
        jnp.asarray(channel_tables()),
        jnp.asarray(position_tables()),
    )
    power = pl.pallas_call(
        interleave,
        out_shape=jax.ShapeDtypeStruct((64, 1024), F32),
        in_specs=[vmem, vmem],
        out_specs=anywhere,
        scratch_shapes=[pltpu.VMEM((512, 128), F32), pltpu.VMEM((64, 1024), F32), dma((8,))],
        compiler_params=pltpu.CompilerParams(vmem_limit_bytes=8 * 1024 * 1024),
    )(arrived, scale)
    return power.reshape(1, 64, 1024)


def solution(mesh):
    return jax.shard_map(
        functools.partial(local, mesh.shape["chan"], mesh.shape["tm"]),
        mesh=mesh,
        in_specs=(P("chan", "tm"), P()),
        out_specs=P("tm", "chan", None),
        check_vma=False,
    )
```

```python
import functools
import math

import jax
import jax.numpy as jnp
import ml_dtypes
import numpy as np
from jax import lax
from jax.experimental import pallas as pl
from jax.experimental.pallas import tpu as pltpu
from jax.sharding import PartitionSpec as P

POSN = 256
CYL = 4
NFFT = 2048
TAPS = 4
TSUM = 4
INPUTS = 1024

STEP = 16
FINE = NFFT // STEP
HALF = FINE // 2
HISTORY = TAPS - 1

BF16 = jnp.bfloat16
F32 = jnp.float32
MESH = pl.DeviceIdType.MESH


def two_parts(table):
    high = table.astype(ml_dtypes.bfloat16)
    low = (table - high.astype(np.float64)).astype(ml_dtypes.bfloat16)
    return np.stack([high, low])


def window_table():
    offsets = np.arange(TAPS * NFFT) + 0.5
    shaped = np.sinc(offsets / NFFT - TAPS / 2.0)
    tapered = 0.5 - 0.5 * np.cos(offsets * (2.0 * math.pi / (TAPS * NFFT)))
    return (shaped * tapered).reshape(TAPS, NFFT).astype(np.float32)


def channel_tables():
    b = np.arange(FINE)[:, None]
    j = np.arange(HALF)[None, :]

    def waves(s):
        angle = 2.0 * math.pi * ((b * (STEP * j + s)) % NFFT) / NFFT
        return np.cos(angle), np.sin(angle)

    out = np.zeros((STEP // 2, 2 * FINE, 2 * FINE))
    for half, s in enumerate((0, STEP // 2)):
        cos, sin = waves(s)
        out[0, half * FINE : (half + 1) * FINE, half * FINE : (half + 1) * FINE] = np.concatenate([cos, -sin], 1)
    for p in range(1, STEP // 2):
        cos, sin = waves(p)
        out[p, :FINE, :FINE] = np.concatenate([cos, -sin], 1)
        out[p, FINE:, :FINE] = np.concatenate([sin, cos], 1)
        cos, sin = waves(STEP - p)
        out[p, :FINE, FINE:] = np.concatenate([cos, -sin], 1)
        out[p, FINE:, FINE:] = np.concatenate([-sin, -cos], 1)
    return two_parts(out / math.sqrt(NFFT))


def position_tables():
    v, r = np.arange(POSN // 2)[:, None], np.arange(POSN // 2)[None, :]
    out = []
    for odd in range(2):
        angle = 2.0 * math.pi * ((v * (2 * r + odd)) % POSN) / POSN
        out.append(np.concatenate(two_parts(np.concatenate([np.cos(angle), np.sin(angle)], 1))))
    return np.stack(out)


def short_dft(x):
    c1, c2, c3 = (math.cos(math.pi * n / 8) for n in (1, 2, 3))
    s = [x[a] + x[a + 8] for a in range(8)]
    d = [x[a] - x[a + 8] for a in range(8)]
    ss = [s[a] + s[a + 4] for a in range(4)]
    sd = [s[a] - s[a + 4] for a in range(4)]
    p0, p1 = ss[0] + ss[2], ss[1] + ss[3]
    t1, t2 = c2 * (sd[1] - sd[3]), c2 * (sd[1] + sd[3])
    f = [None] + [d[a] - d[8 - a] for a in (1, 2, 3)]
    g = [None] + [d[a] + d[8 - a] for a in (1, 2, 3)]
    cf, cg = c2 * f[2], c2 * g[2]
    even, odd = d[0] + cf, d[0] - cf
    pp, qq = c1 * f[1] + c3 * f[3], c3 * f[1] - c1 * f[3]
    vv, ww = c3 * g[1] + c1 * g[3], c1 * g[1] - c3 * g[3]
    ee, ff = cg + d[4], cg - d[4]
    return [
        (p0 + p1, p0 - p1),
        (even + pp, -(vv + ee)),
        (sd[0] + t1, -(sd[2] + t2)),
        (odd + qq, -(ww + ff)),
        (ss[0] - ss[2], ss[3] - ss[1]),
        (odd - qq, ff - ww),
        (sd[0] - t1, sd[2] - t2),
        (even - pp, ee - vv),
    ]


def dot(left, right):
    return jnp.dot(left, right, preferred_element_type=F32)


def kernel(
    peers,
    blocks,
    samples,
    cell_in,
    window_in,
    channel_in,
    position_in,
    arrived,
    scale_in,
    frames,
    cell,
    window,
    channel,
    position,
    terms,
    outgoing,
    spectra,
    choose,
    along,
    energy,
    packed,
    scale_out,
    load_sem,
    halo_send,
    halo_recv,
    spectra_send,
    spectra_recv,
    power_send,
    power_recv,
    scale_send,
    scale_recv,
    around,
):
    me = lax.axis_index("chan")
    block = lax.axis_index("tm")
    is_first, is_last = block == 0, block == blocks - 1

    def device(flip, dy):
        return lax.rem(me // 8 + flip, 2) * 8 + lax.rem(lax.rem(me, 8) + 8 + dy, 8)

    def near(k):
        place = lax.rem(k + 2, 10)
        return device(place // 5, lax.rem(place, 5) - 2)

    def far(k):
        return device(k // 3, lax.rem(k, 3) + 3)

    def drained(ref, sem):
        pltpu.make_async_copy(ref, ref, sem).wait()

    for q in range(TSUM):
        pltpu.make_async_copy(
            samples.at[:, pl.ds(q * NFFT, NFFT)], frames.at[HISTORY + q], load_sem.at[0]
        ).start()
    loads = [
        pltpu.make_async_copy(source, target, load_sem.at[n + 1])
        for n, (source, target) in enumerate(
            ((window_in, window), (channel_in, channel), (position_in, position), (cell_in, cell))
        )
    ]
    for load in loads:
        load.start()

    barrier = pltpu.get_barrier_semaphore()

    @pl.when(jnp.logical_not(is_first))
    def _():
        pl.semaphore_signal(barrier, inc=1, device_id={"tm": block - 1}, device_id_type=MESH)

    def greet(k, carry):
        pl.semaphore_signal(barrier, inc=1, device_id={"chan": near(k)}, device_id_type=MESH)
        return carry

    lax.fori_loop(1, 10, greet, 0)

    def halo(f):
        return pltpu.make_async_remote_copy(
            src_ref=samples.at[:, pl.ds((f + 1) * NFFT, NFFT)],
            dst_ref=frames.at[f],
            send_sem=halo_send,
            recv_sem=halo_recv.at[f],
            device_id={"tm": block + 1},
            device_id_type=MESH,
        )

    def spectra_copy(t, target):
        return pltpu.make_async_remote_copy(
            src_ref=outgoing.at[t, target],
            dst_ref=spectra.at[t, me],
            send_sem=spectra_send,
            recv_sem=spectra_recv.at[t],
            device_id={"chan": target},
            device_id_type=MESH,
        )

    def power_copy(target):
        return pltpu.make_async_remote_copy(
            src_ref=packed.at[target],
            dst_ref=arrived.at[me],
            send_sem=power_send,
            recv_sem=power_recv,
            device_id={"chan": target},
            device_id_type=MESH,
        )

    def scale_copy(target):
        return pltpu.make_async_remote_copy(
            src_ref=scale_out.at[target],
            dst_ref=scale_in.at[me],
            send_sem=scale_send,
            recv_sem=scale_recv,
            device_id={"chan": target},
            device_id_type=MESH,
        )

    def filter_frame(t):
        def rows_of(r, carry):
            rows = pl.ds(pl.multiple_of(r * 16, 16), 16)
            x = []
            for a in range(STEP):
                lanes = pl.ds(a * FINE, FINE)
                total = None
                for k in range(TAPS):
                    term = window[pl.ds(k, 1), lanes] * frames[t + k, rows, lanes].astype(F32)
                    total = term if total is None else total + term
                x.append(total)
            for p, pair in enumerate(short_dft(x)):
                for part, value in enumerate(pair):
                    lanes = pl.ds(part * FINE, FINE)
                    high = value.astype(BF16)
                    terms[p, rows, lanes] = high
                    terms[p, pl.ds(pl.multiple_of(64 + r * 16, 16), 16), lanes] = (value - high.astype(F32)).astype(BF16)
            return carry

        lax.fori_loop(0, 4, rows_of, 0)

    def channelize(t):
        for p in range(STEP // 2):
            first = dot(terms[p], channel[0, p])
            second = dot(terms[p, pl.ds(0, 64), :], channel[1, p])
            result = (first[:64] + first[64:] + second).astype(BF16)
            outgoing[t, p] = result[:, :FINE]
            outgoing[t, 8 if p == 0 else STEP - p] = result[:, FINE:]

    def send_near(t):
        def one(k, carry):
            spectra_copy(t, near(k)).start()
            return carry

        lax.fori_loop(1, 10, one, 0)

    def send_far(t):
        def one(k, carry):
            spectra_copy(t, far(k)).start()
            return carry

        lax.fori_loop(0, 6, one, 0)
        spectra[t, me] = outgoing[t, me]

    drained(frames.at[pl.ds(HISTORY, TSUM)], load_sem.at[0])
    loads[0].wait()
    filter_frame(TSUM - 1)
    loads[1].wait()
    channelize(TSUM - 1)
    pl.semaphore_wait(barrier, jnp.where(is_last, 9, 10))
    for dy in (2, 6):
        pl.semaphore_signal(around, inc=1, device_id={"chan": device(0, dy)}, device_id_type=MESH)

    @pl.when(jnp.logical_not(is_last))
    def _():
        for f in (2, 1, 0):
            halo(f).start()

    send_near(TSUM - 1)
    pl.semaphore_wait(around, 2)
    send_far(TSUM - 1)

    loads[3].wait()

    def choose_rows(r, carry):
        first = pl.multiple_of(r * 32, 32)
        base = first // POSN * POSN + lax.rem(first, POSN // 2) * 2 + lax.rem(first // (POSN // 2), 2)
        number = lax.broadcasted_iota(jnp.int32, (32, INPUTS), 0) * 2 + base
        choose[pl.ds(first, 32), :] = jnp.where(number == cell[...], 1.0, 0.0).astype(BF16)
        return carry

    lax.fori_loop(0, INPUTS // 32, choose_rows, 0)

    def later_frame(step, carry):
        t = TSUM - 1 - step

        @pl.when(jnp.logical_not(is_first))
        def _():
            halo(t).wait_recv()

        @pl.when(is_first)
        def _():
            frames[t] = jnp.zeros((64, NFFT), BF16)

        filter_frame(t)
        channelize(t)
        send_far(t)
        send_near(t)
        return carry

    lax.fori_loop(1, TSUM, later_frame, 0)

    loads[2].wait()
    lane = lax.broadcasted_iota(jnp.int32, (1, FINE), 1)
    left = lane < HALF
    sign = jnp.where(left, 1.0, -1.0)

    def turned(value):
        return pltpu.roll(value, HALF, 1) * sign

    def beams_of(group):
        for t in group:
            drained(spectra.at[t, pl.ds(0, peers - 1)], spectra_recv.at[t])
        received = jnp.concatenate([spectra[t].reshape(INPUTS, FINE) for t in group], axis=1)
        half = POSN // 2
        for g in range(CYL):
            placed = dot(choose[pl.ds(g * POSN, POSN), :], received)
            swapped = jnp.concatenate([turned(placed[:, n * FINE : (n + 1) * FINE]) for n in range(len(group))], axis=1)
            sums = []
            for odd in range(2):
                rows = slice(odd * half, (odd + 1) * half)
                both = jnp.concatenate([placed[rows], swapped[rows]], axis=0).astype(BF16)
                parts = dot(position[odd], both)
                sums.append(parts[:half] + parts[half:])
            along[g, :half, : len(group) * FINE] = sums[0] + sums[1]
            along[g, half:, : len(group) * FINE] = sums[0] - sums[1]

    def power_of(group, first):
        def power_rows(r, carry):
            rows = pl.ds(pl.multiple_of(r * 32, 32), 32)
            squares = [None] * CYL
            for n in range(len(group)):
                a = [along[g, rows, pl.ds(n * FINE, FINE)] for g in range(CYL)]
                even, odd = a[0] + a[2], a[1] + a[3]
                across, quarter = a[0] - a[2], turned(a[1] - a[3])
                for u, beam in enumerate((even + odd, across + quarter, even - odd, across - quarter)):
                    squares[u] = beam * beam if n == 0 else squares[u] + beam * beam
            for duo in range(2):
                one, two = squares[2 * duo], squares[2 * duo + 1]
                folded = jnp.where(left, one, two) + pltpu.roll(jnp.where(left, two, one), HALF, 1)
                folded = folded if first else energy[duo, rows, :] + folded
                energy[duo, rows, :] = folded
                carry = jnp.maximum(carry, jnp.max(folded.reshape(-1, 8, FINE), axis=0))
            return carry

        return lax.fori_loop(0, POSN // 32, power_rows, jnp.zeros((8, FINE), F32), unroll=8)

    for n, group in enumerate(((3, 2), (1,), (0,))):
        beams_of(group)
        heights = power_of(group, n == 0)

    largest = jnp.max(jnp.max(heights, axis=0, keepdims=True), axis=1, keepdims=True)
    largest = jnp.maximum(largest, 1e-36)
    scale_out[...] = jnp.broadcast_to((largest * (1.0 / (TSUM * INPUTS))).reshape(1, 1, 1), (peers, 1, 128))
    inverse = 1.0 / largest

    for duo in range(2):
        for side in range(2):
            share = energy[duo, pl.ds(side * 128, 128), :] * inverse
            share = share * share
            upright = (share * share).T
            for u in range(2):
                low = upright[u * HALF : u * HALF + 32]
                high = upright[u * HALF + 32 : u * HALF + 64]
                target = (2 * duo + u) * 4 + 2 * side
                packed[target] = jnp.where(left, low, pltpu.roll(high, HALF, 1)).astype(BF16)
                packed[target + 1] = jnp.where(left, pltpu.roll(low, HALF, 1), high).astype(BF16)

    def send_power(which, first, last):
        def blocks_of(k, carry):
            power_copy(which(k)).start()
            return carry

        def scales_of(k, carry):
            scale_copy(which(k)).start()
            return carry

        lax.fori_loop(first, last, blocks_of, 0)
        lax.fori_loop(first, last, scales_of, 0)

    send_power(far, 0, 6)
    send_power(near, 1, 10)
    arrived[me] = packed[me]
    scale_in[me] = scale_out[me]

    @pl.when(jnp.logical_not(is_last))
    def _():
        drained(frames.at[pl.ds(0, HISTORY)], halo_send)

    others = pl.ds(0, peers - 1)
    drained(outgoing.at[:, others], spectra_send)
    drained(packed.at[others], power_send)
    drained(scale_out.at[others], scale_send)
    drained(arrived.at[others], power_recv)
    drained(scale_in.at[others], scale_recv)


def interleave(arrived, scale, out, ordered, ready, sem):
    copies = []
    for q in range(4):
        for s in range(STEP if q % 2 == 0 else 0):
            value = arrived[s, pl.ds(8 * q, 16), :].astype(F32)
            ordered[pl.ds(q * 128 + s, 16, stride=STEP), :] = lax.rsqrt(lax.rsqrt(value)) * scale[s]
        upright = ordered[pl.ds(q * 128, 128), :].T
        for high in range(2):
            lanes = pl.ds(512 * high + 128 * q, 128)
            ready[:, lanes] = upright[HALF * high : HALF * (high + 1)]
            copies.append(pltpu.make_async_copy(ready.at[:, lanes], out.at[:, lanes], sem.at[2 * q + high]))
            copies[-1].start()
    for copy in copies:
        copy.wait()


def local(peers, blocks, samples, cell_of_feed):
    vmem = pl.BlockSpec(memory_space=pltpu.VMEM)
    anywhere = pl.BlockSpec(memory_space=pl.ANY)
    dma = pltpu.SemaphoreType.DMA
    arrived, scale = pl.pallas_call(
        functools.partial(kernel, peers, blocks),
        out_shape=(
            pltpu.VMEM((peers, 32, 128), BF16),
            pltpu.VMEM((peers, 1, 128), F32),
        ),
        in_specs=[anywhere] * 5,
        out_specs=(vmem, vmem),
        scratch_shapes=[
            pltpu.VMEM((HISTORY + TSUM, 64, NFFT), BF16),
            pltpu.VMEM((1, INPUTS), jnp.int32),
            pltpu.VMEM((TAPS, NFFT), F32),
            pltpu.VMEM((2, STEP // 2, 2 * FINE, 2 * FINE), BF16),
            pltpu.VMEM((2, POSN, POSN), BF16),
            pltpu.VMEM((STEP // 2, 128, 2 * FINE), BF16),
            pltpu.VMEM((TSUM, peers, 64, FINE), BF16),
            pltpu.VMEM((TSUM, peers, 64, FINE), BF16),
            pltpu.VMEM((INPUTS, INPUTS), BF16),
            pltpu.VMEM((CYL, POSN, 2 * FINE), F32),
            pltpu.VMEM((2, POSN, FINE), F32),
            pltpu.VMEM((peers, 32, 128), BF16),
            pltpu.VMEM((peers, 1, 128), F32),
            dma((5,)),
            dma(()),
            dma((HISTORY,)),
            dma(()),
            dma((TSUM,)),
            dma(()),
            dma(()),
            dma(()),
            dma(()),
            pltpu.SemaphoreType.REGULAR,
        ],
        compiler_params=pltpu.CompilerParams(
            collective_id=0, has_side_effects=True, vmem_limit_bytes=60 * 1024 * 1024
        ),
    )(
        samples,
        cell_of_feed.reshape(1, INPUTS),
        jnp.asarray(window_table()),
        jnp.asarray(channel_tables()),
        jnp.asarray(position_tables()),
    )
    power = pl.pallas_call(
        interleave,
        out_shape=jax.ShapeDtypeStruct((64, 1024), F32),
        in_specs=[vmem, vmem],
        out_specs=anywhere,
        scratch_shapes=[pltpu.VMEM((512, 128), F32), pltpu.VMEM((64, 1024), F32), dma((8,))],
        compiler_params=pltpu.CompilerParams(vmem_limit_bytes=8 * 1024 * 1024),
    )(arrived, scale)
    return power.reshape(1, 64, 1024)


def solution(mesh):
    return jax.shard_map(
        functools.partial(local, mesh.shape["chan"], mesh.shape["tm"]),
        mesh=mesh,
        in_specs=(P("chan", "tm"), P()),
        out_specs=P("tm", "chan", None),
        check_vma=False,
    )
```
